256 devices in a mesh: dap: 16 (over x_hi, z), dp: 16 (over y, x_lo, core).
Axes of the slice: x: 4 (x_hi: 2, x_lo: 2; x = x_hi * 2 + x_lo), y: 4, z: 8, core: 2. Of those that a mesh axis runs over, the one named last changes fastest.
Arguments:
- alignment: bfloat16 [2048, 256, 256], P(('dp', 'dap')), parts along dimension 0, may hold values from -6 to 6
- pair_state: bfloat16 [4096, 256, 128], P(('dp', 'dap')), parts along dimension 0, may hold values from -6 to 6
- residue_present_mask: int32 [4096], P('dp'), parts along dimension 0, may hold values 0 or 1
- alignment_row_mask: int32 [2048], P('dp'), parts along dimension 0, may hold values 0 or 1
- row_query_weight: bfloat16 [256, 256], replicated
- row_key_weight: bfloat16 [256, 256], replicated
- row_value_weight: bfloat16 [256, 256], replicated, may hold values from -0.375 to 0.375
- row_gate_weight: bfloat16 [256, 256], replicated, may hold values from -0.375 to 0.375
- row_output_weight: bfloat16 [256, 256], replicated, may hold values from -1 to 1
- pair_bias_weight: bfloat16 [128, 8], replicated, may hold values from -1.1953125 to 1.1953125
- column_query_weight: bfloat16 [256, 256], replicated
- column_key_weight: bfloat16 [256, 256], replicated
- column_value_weight: bfloat16 [256, 256], replicated, may hold values from -0.375 to 0.375
- column_gate_weight: bfloat16 [256, 256], replicated, may hold values from -0.375 to 0.375
- column_output_weight: bfloat16 [256, 256], replicated, may hold values from -1 to 1
- triangle_left_weight: bfloat16 [128, 128], replicated, may hold values from -0.5 to 0.5
- triangle_right_weight: bfloat16 [128, 128], replicated, may hold values from -0.5 to 0.5
- triangle_gate_weight: bfloat16 [128, 128], replicated, may hold values from -0.5 to 0.5
- triangle_output_weight: bfloat16 [128, 128], replicated, may hold values from -0.5 to 0.5
- transition_input_weight: bfloat16 [128, 512], replicated, may hold values from -0.5 to 0.5
- transition_output_weight: bfloat16 [512, 128], replicated, may hold values from -0.25 to 0.25
Outputs:
- alignment_updated: bfloat16 [2048, 256, 256], P('dp', 'dap'), parts along dimension 0
- pair_next: bfloat16 [4096, 256, 128], P(('dp', 'dap')), parts along dimension 0
The draws below stay inside these ranges and needn't reach their ends.
There are 16 independent parts, one for each index of `dp`. The reference program is written for one: setup_inputs(seed, part) draws one part's arguments, and reference() takes and returns one part's arrays. A program takes and returns all parts, laid end to end along the dimension named above; an argument that names none is the same for every part. Nothing has to cross between parts.
All inputs are finite; a program needn't handle non-finite values.
Results may differ from the reference program's by a relative error of at most 0.012.
The reference program's roundings to bfloat16 on the way count: a program that leaves them out, or rounds other values in their place, can miss the bound.
Values may be sent and summed in bfloat16 or wider, within the bound.
A program may use at most 128 MiB of HBM per device.

```python
import jax
import jax.numpy as jnp
from jax import lax

CM = 256
CZ = 128
HM = 8
DH = 32
CT = 128
PT = 512
RES = 256
SEQUENCE_ROWS = 128


def paired_weights(key, offset, in_width, head_count, lowest, highest):
    key = jax.random.fold_in(key, offset)
    first_key, second_key, third_key = jax.random.split(key, 3)
    shape = (in_width, head_count, DH)
    queries = jax.random.normal(first_key, shape, jnp.float32) * in_width ** (-0.5)
    others = jax.random.normal(second_key, shape, jnp.float32) * in_width ** (-0.5)
    strength = jax.random.uniform(third_key, (1, head_count, 1), jnp.float32, lowest, highest)
    queries = queries * strength
    key_weights = strength * others
    return (queries.reshape(in_width, head_count * DH), key_weights.reshape(in_width, head_count * DH))


def draw_row_query_weight(key, part):
    weight_pair = paired_weights(key, 17, CM, HM, 1.0, 1.0)
    return weight_pair[0].astype(jnp.bfloat16)


def draw_row_key_weight(key, part):
    weight_pair = paired_weights(key, 17, CM, HM, 1.0, 1.0)
    return weight_pair[1].astype(jnp.bfloat16)


def draw_column_query_weight(key, part):
    weight_pair = paired_weights(key, 29, CM, HM, 1.0, 1.0)
    return weight_pair[0].astype(jnp.bfloat16)


def draw_column_key_weight(key, part):
    weight_pair = paired_weights(key, 29, CM, HM, 1.0, 1.0)
    return weight_pair[1].astype(jnp.bfloat16)


def place_ends(entries, key, low, largest):
    dims = entries.shape
    spot = [jax.random.randint(jax.random.fold_in(key, axis), (), 0, dims[axis]) for axis in range(len(dims))]
    entries = entries.at[tuple(spot)].set(low)
    longest = dims.index(max(dims))
    spot[longest] = (spot[longest] + 1) % dims[longest]
    return entries.at[tuple(spot)].set(largest)


def block_scale(rng, shape, cuts, low, top_value):
    level, own = 1.0, jax.random.fold_in(rng, 6)
    for axis_at, parts in cuts:
        steps = jnp.exp(jax.random.uniform(jax.random.fold_in(own, axis_at), (parts,), jnp.float32, low / len(cuts), top_value / len(cuts)))
        level = level * jnp.repeat(steps, shape[axis_at] // parts).reshape([-1 if axis == axis_at else 1 for axis in range(len(shape))])
    return level


def centred(rng, shape, spread, limit, cuts=(), kind=jnp.bfloat16):
    level = block_scale(rng, shape, cuts, -0.22, 0.18) if cuts else 1.0
    array = jax.random.normal(rng, shape, jnp.float32) * spread * level
    return jnp.minimum(jnp.maximum(array, -limit), limit).astype(kind)


def setup_inputs(seed: int = 0, part: int = 0) -> dict:
    splits = jax.random.split(jax.random.key(seed), 22)
    part_splits = jax.random.split(jax.random.fold_in(splits[21], part), 22)
    alignment = centred(part_splits[0], (SEQUENCE_ROWS, RES, CM), 1.0, 6.0, ((0, 16),))
    pair_state = centred(part_splits[1], (RES, RES, CZ), 1.0, 6.0, ((0, 16),))
    residue_present_mask = place_ends((jax.random.randint(part_splits[2], (RES,), 0, 8) < 7).astype(jnp.int32), jax.random.fold_in(part_splits[2], 1), 0, 1)
    alignment_row_mask = place_ends((jax.random.randint(part_splits[3], (SEQUENCE_ROWS,), 0, 8) < 7).astype(jnp.int32), jax.random.fold_in(part_splits[3], 1), 0, 1)
    row_query_weight = draw_row_query_weight(jax.random.fold_in(splits[21], 71), part)
    row_key_weight = draw_row_key_weight(jax.random.fold_in(splits[21], 71), part)
    row_value_weight = centred(splits[6], (CM, HM * DH), CM ** -0.5, 0.375)
    row_gate_weight = centred(splits[7], (CM, HM * DH), CM ** -0.5, 0.375)
    row_output_weight = centred(splits[8], (HM * DH, CM), DH ** -0.5, 1.0)
    pair_bias_weight = centred(splits[9], (CZ, HM), 0.2, 1.1953125)
    column_query_weight = draw_column_query_weight(jax.random.fold_in(splits[21], 71), part)
    column_key_weight = draw_column_key_weight(jax.random.fold_in(splits[21], 71), part)
    column_value_weight = centred(splits[12], (CM, HM * DH), CM ** -0.5, 0.375)
    column_gate_weight = centred(splits[13], (CM, HM * DH), CM ** -0.5, 0.375)
    column_output_weight = centred(splits[14], (HM * DH, CM), DH ** -0.5, 1.0)
    triangle_left_weight = centred(splits[15], (CZ, CT), CZ ** -0.5, 0.5)
    triangle_right_weight = centred(splits[16], (CZ, CT), CZ ** -0.5, 0.5)
    triangle_gate_weight = centred(splits[17], (CZ, CZ), CZ ** -0.5, 0.5)
    triangle_output_weight = centred(splits[18], (CT, CZ), CT ** -0.5, 0.5)
    transition_input_weight = centred(splits[19], (CZ, PT), CZ ** -0.5, 0.5)
    transition_output_weight = centred(splits[20], (PT, CZ), PT ** -0.5, 0.25)
    return {"alignment": alignment, "pair_state": pair_state, "residue_present_mask": residue_present_mask, "alignment_row_mask": alignment_row_mask, "row_query_weight": row_query_weight, "row_key_weight": row_key_weight, "row_value_weight": row_value_weight, "row_gate_weight": row_gate_weight, "row_output_weight": row_output_weight, "pair_bias_weight": pair_bias_weight, "column_query_weight": column_query_weight, "column_key_weight": column_key_weight, "column_value_weight": column_value_weight, "column_gate_weight": column_gate_weight, "column_output_weight": column_output_weight, "triangle_left_weight": triangle_left_weight, "triangle_right_weight": triangle_right_weight, "triangle_gate_weight": triangle_gate_weight, "triangle_output_weight": triangle_output_weight, "transition_input_weight": transition_input_weight, "transition_output_weight": transition_output_weight}


epsilon = 1e-05
masked_score = -1000000000.0

def layer_normalize(values):
    values = values.astype(jnp.float32)
    center = values - lax.optimization_barrier(jnp.mean(values, axis=-1, keepdims=True))
    variance = lax.optimization_barrier(jnp.mean(center * center, axis=-1, keepdims=True))
    return (center * lax.rsqrt(variance + epsilon)).astype(jnp.bfloat16)

def project(values, weight):
    flattened = values.reshape(-1, values.shape[-1])
    result = jnp.dot(flattened, weight, preferred_element_type=jnp.float32)
    return result.reshape(values.shape[:-1] + (weight.shape[1],))

def gated_head_attention(normalized_input, bias_term, key_bias, w_query, w_key, w_value, w_gate, w_out):
    length = normalized_input.shape[0]
    head_count = w_query.shape[1] // DH
    query_rows = (project(normalized_input, w_query) * DH ** (-0.5)).astype(jnp.bfloat16).reshape(length, head_count, DH)
    key_rows = project(normalized_input, w_key).astype(jnp.bfloat16).reshape(length, head_count, DH)
    value_rows = project(normalized_input, w_value).astype(jnp.bfloat16).reshape(length, head_count, DH)
    gate_rows = jax.nn.sigmoid(project(normalized_input, w_gate))
    scores = jnp.einsum('ihd,jhd->hij', query_rows.astype(jnp.float32), key_rows.astype(jnp.float32))
    scores = scores + bias_term + key_bias[None, None, :]
    row_max = lax.optimization_barrier(jnp.max(scores, axis=-1, keepdims=True))
    expo = jnp.exp(scores - row_max)
    row_total = lax.optimization_barrier(jnp.sum(expo, axis=-1, keepdims=True))
    probabilities = (expo / row_total).astype(jnp.bfloat16)
    mixture = jnp.einsum('hij,jhd->ihd', probabilities.astype(jnp.float32), value_rows.astype(jnp.float32))
    gated_rows = (mixture.reshape(length, head_count * DH) * gate_rows).astype(jnp.bfloat16)
    return jnp.dot(gated_rows, w_out, preferred_element_type=jnp.float32)

def reference(alignment, pair_state, residue_present_mask, alignment_row_mask, row_query_weight, row_key_weight, row_value_weight, row_gate_weight, row_output_weight, pair_bias_weight, column_query_weight, column_key_weight, column_value_weight, column_gate_weight, column_output_weight, triangle_left_weight, triangle_right_weight, triangle_gate_weight, triangle_output_weight, transition_input_weight, transition_output_weight):
    residue_live = residue_present_mask.astype(jnp.float32)
    sequence_present = alignment_row_mask.astype(jnp.float32)
    residue_mask_bias = (1.0 - residue_live) * masked_score
    seq_bias = (1.0 - sequence_present) * masked_score
    pair_norm = layer_normalize(pair_state)
    pair_bias = jnp.transpose(project(pair_norm, pair_bias_weight), (2, 0, 1)).astype(jnp.bfloat16)
    bias_expanded = pair_bias.astype(jnp.float32)
    alignment_normalized = layer_normalize(alignment)
    row_attention_update = lax.map(lambda normalized_input: gated_head_attention(normalized_input, bias_expanded, residue_mask_bias, row_query_weight, row_key_weight, row_value_weight, row_gate_weight, row_output_weight), alignment_normalized)
    alignment_middle = (alignment.astype(jnp.float32) + row_attention_update).astype(jnp.bfloat16)
    column_normalize = layer_normalize(jnp.transpose(alignment_middle, (1, 0, 2)))
    column_attention_update = lax.map(lambda normalized_input: gated_head_attention(normalized_input, 0.0, seq_bias, column_query_weight, column_key_weight, column_value_weight, column_gate_weight, column_output_weight), column_normalize)
    alignment_updated = (alignment_middle.astype(jnp.float32) + jnp.transpose(column_attention_update, (1, 0, 2))).astype(jnp.bfloat16)
    pair_live = residue_live[:, None] * residue_live[None, :]
    left = (project(pair_norm, triangle_left_weight) * pair_live[:, :, None]).astype(jnp.bfloat16)
    right = (project(pair_norm, triangle_right_weight) * pair_live[:, :, None]).astype(jnp.bfloat16)
    left_wide = jnp.transpose(left, (2, 0, 1)).astype(jnp.float32)
    right_wide = jnp.transpose(right, (2, 0, 1)).astype(jnp.float32)
    combined = jnp.einsum('cik,cjk->cij', left_wide, right_wide)
    combined_norm = layer_normalize(jnp.transpose(combined, (1, 2, 0)))
    gate_values = jax.nn.sigmoid(project(pair_norm, triangle_gate_weight))
    pair_mid = (pair_state.astype(jnp.float32) + project(combined_norm, triangle_output_weight) * gate_values).astype(jnp.bfloat16)
    trans_norm = layer_normalize(pair_mid)
    hidden = jax.nn.relu(project(trans_norm, transition_input_weight)).astype(jnp.bfloat16)
    pair_next = (pair_mid.astype(jnp.float32) + project(hidden, transition_output_weight)).astype(jnp.bfloat16)
    return (alignment_updated, pair_next)
```

```python
import functools

import jax
import jax.numpy as jnp
from jax import lax
from jax.experimental import pallas as pl
from jax.experimental.pallas import tpu as pltpu
from jax.sharding import PartitionSpec as P

MESH = pl.DeviceIdType.MESH
F32 = jnp.float32
BF16 = jnp.bfloat16
N = 16
HEADS = 8
DH = 32
EPSILON = 1e-05
MASKED = -1000000000.0


def mm(a, b):
    return jnp.dot(a, b, preferred_element_type=F32)


def nt(a, b):
    return lax.dot_general(a, b, (((1,), (1,)), ((), ())), preferred_element_type=F32)


def tn(a, b):
    return lax.dot_general(a, b, (((0,), (0,)), ((), ())), preferred_element_type=F32)


def normalize(x):
    center = x - jnp.mean(x, axis=-1, keepdims=True)
    variance = jnp.mean(center * center, axis=-1, keepdims=True)
    return (center * lax.rsqrt(variance + EPSILON)).astype(BF16)


def sigmoid(x):
    return 1.0 / (1.0 + jnp.exp(-x))


def transposed(w):
    return jnp.transpose(w.astype(F32)).astype(BF16)


def attend(k_rows, qz, vt, gt, bias, heads, width, store):
    scores = mm(k_rows, qz) + bias
    top = jnp.max(scores, axis=0, keepdims=True)
    weights = jnp.exp(scores - top).astype(BF16)
    for n, h in enumerate(heads):
        part = weights if len(heads) == 1 else weights[:, n * width : (n + 1) * width]
        mix = mm(vt[h], part)
        gated = mix[:DH] * (1.0 / mix[DH : DH + 1]) * gt[h * DH : (h + 1) * DH]
        store(h, gated.astype(BF16))


def kernel(
    al, pr, rmask_s, rmask, smask,
    rwq, rwk, rwv, rwg, rwo, pbw, cwq, cwk, cwv, cwg, cwo, tlw, trw, tgw, tow, tiw, tww,
    out_al, out_pr,
    pn, lr_t, b_t, send_lr, recv_lr, send_b, recv_b, bias_t, send_m, recv_m, send_c, recv_c,
    wt, wlr, wb, qz, vt, qzc, vtc, gt, gtc, cn, gcol, cnt, gate, swap, eye,
    s_lr, r_lr, s_b, r_b, s_m, r_m, s_c, r_c,
):
    me = lax.axis_index("dap")

    def peer(o):
        return lax.rem(me + o, N)

    barrier = pltpu.get_barrier_semaphore()
    for o in range(1, N):
        pl.semaphore_signal(barrier, inc=1, device_id={"dap": peer(o)}, device_id_type=MESH)

    def copy(src, dst, ssem, rsem, to):
        return pltpu.make_async_remote_copy(
            src_ref=src, dst_ref=dst, send_sem=ssem, recv_sem=rsem,
            device_id={"dap": to}, device_id_type=MESH,
        )

    def send_to(send, recv, ssem, rsem, d):
        return copy(send.at[d], recv.at[me], ssem.at[d], rsem.at[me], d)

    def arrival(send, recv, ssem, rsem, d):
        return copy(send.at[d], recv.at[d], ssem.at[d], rsem.at[d], d)

    def wait_all(send, recv, ssem, rsem):
        @pl.loop(1, N)
        def _(o):
            arrival(send, recv, ssem, rsem, peer(o)).wait_recv()

    row = lax.broadcasted_iota(jnp.int32, (256, 256), 0)
    col = lax.broadcasted_iota(jnp.int32, (256, 256), 1)
    swap[...] = jnp.where(col == (row % 16) * 16 + row // 16, 1.0, 0.0).astype(BF16)
    eye[...] = jnp.where(col == row, 1.0, 0.0).astype(BF16)

    wlr[:128, :] = transposed(tlw[...])
    wlr[128:, :] = transposed(trw[...])
    wb[...] = jnp.zeros_like(wb)
    wb[:, :HEADS] = pbw[...].astype(F32)
    wbt = jnp.transpose(wb[...])[:16].astype(BF16)
    live = rmask[...].astype(F32)

    @pl.loop(0, 16)
    def _(i):
        normed = normalize(pr[i].astype(F32))
        pn[i] = normed
        own = rmask_s[me * 16 + i].astype(F32)
        lr_t[i] = (nt(wlr[...], normed) * (live * own)).astype(BF16)
        b_t[i] = nt(wbt, normed).astype(BF16)

    send_b[...] = mm(swap[...], b_t[...].reshape(256, 256))[:128].astype(BF16).reshape(8, 16, 256)

    pl.semaphore_wait(barrier, N - 1)

    def send_bias(d):
        return copy(send_b, recv_b.at[me], s_b.at[d], r_b.at[me], d)

    for o in range(1, N):
        send_bias(peer(o)).start()
    recv_b[me] = send_b[...]

    def split_group(g):
        at = pl.multiple_of(g * 16, 16)
        for side in range(2):
            block = lr_t[:, pl.ds(side * 128 + at, 16), :].reshape(256, 256)
            swapped = mm(swap[...], block).astype(BF16).reshape(2, 8, 16, 256)
            send_lr[2 * g, side] = swapped[0]
            send_lr[2 * g + 1, side] = swapped[1]

    @pl.loop(1, 8)
    def _(n):
        g = lax.rem(me // 2 + n, 8)
        split_group(g)
        send_to(send_lr, recv_lr, s_lr, r_lr, 2 * g).start()
        send_to(send_lr, recv_lr, s_lr, r_lr, 2 * g + 1).start()

    split_group(me // 2)
    near = me + 1 - 2 * (me % 2)
    send_to(send_lr, recv_lr, s_lr, r_lr, near).start()
    recv_lr[me] = send_lr[me]

    wt[0] = transposed(rwq[...])
    wt[1] = transposed(rwv[...])
    wt[2] = transposed(rwg[...])
    wt[3] = transposed(cwq[...])
    wt[4] = transposed(cwv[...])
    wt[5] = transposed(cwg[...])
    qz[...] = jnp.zeros_like(qz)
    qzc[...] = jnp.zeros_like(qzc)
    vt[:, DH:, :] = jnp.ones((HEADS, 16, 256), BF16)
    vtc[:, DH:, :] = jnp.ones((HEADS, 16, 128), BF16)

    @pl.loop(0, 16)
    def _(i):
        gate[i] = sigmoid(mm(pn[i], tgw[...]))

    wait_all(recv_b, recv_b, s_b, r_b)
    shown = nt(eye[...], jnp.broadcast_to(live, (256, 256)).astype(BF16))
    hidden_keys = (1.0 - shown) * MASKED

    @pl.loop(0, HEADS)
    def _(h):
        bias_t[h] = nt(eye[...], recv_b[:, h].reshape(256, 256)) + hidden_keys

    scale = DH ** (-0.5)

    @pl.loop(0, 8)
    def _(s):
        normed = normalize(al[s].astype(F32))
        q = (nt(wt[0], normed) * scale).astype(BF16)
        v = nt(wt[1], normed).astype(BF16)
        g = sigmoid(nt(wt[2], normed))
        k = mm(normed, rwk[...]).astype(BF16)
        for h in range(HEADS):
            qz[h, h * DH : (h + 1) * DH, :] = q[h * DH : (h + 1) * DH]
            vt[h, :DH, :] = v[h * DH : (h + 1) * DH]

        def store(h, gated):
            gt[h * DH : (h + 1) * DH, :] = gated

        for h in range(HEADS):
            attend(k, qz[h], vt, g, bias_t[h], (h,), 256, store)
        mid = (al[s].astype(F32) + tn(gt[...], rwo[...])).astype(BF16)
        send_m[:, s] = mid.reshape(16, 16, 256)

    for o in range(1, N):
        send_to(send_m, recv_m, s_m, r_m, peer(o)).start()
    recv_m[me] = send_m[me]

    wait_all(send_lr, recv_lr, s_lr, r_lr)

    @pl.loop(0, 8)
    def _(c):
        left = recv_lr[:, 0, c].reshape(256, 256)
        right = recv_lr[:, 1, c].reshape(256, 256)
        send_c[:, c] = nt(left, right).astype(BF16).reshape(16, 16, 256)

    for o in range(1, N):
        send_to(send_c, recv_c, s_c, r_c, peer(o)).start()
    recv_c[me] = send_c[me]

    wait_all(send_m, recv_m, s_m, r_m)

    @pl.loop(0, 8)
    def _(b):
        rows = recv_m[pl.ds(2 * b, 2)].reshape(256, 256).astype(F32)
        at = pl.multiple_of(b * 16, 16)
        cn[:, pl.ds(at, 16), :] = mm(swap[...], normalize(rows)).astype(BF16).reshape(16, 16, 256)

    seen = nt(eye[:128, :128], jnp.broadcast_to(smask[...].astype(F32), (256, 128)).astype(BF16))
    hidden_rows = (1.0 - seen) * MASKED

    @pl.loop(0, 16)
    def _(i):
        normed = cn[i]
        q = (nt(wt[3], normed) * scale).astype(BF16)
        v = nt(wt[4], normed).astype(BF16)
        g = sigmoid(nt(wt[5], normed))
        k = mm(normed, cwk[...]).astype(BF16)
        for h in range(HEADS):
            side = (h % 2) * 128
            qzc[h // 2, h * DH : (h + 1) * DH, side : side + 128] = q[h * DH : (h + 1) * DH]
            vtc[h, :DH, :] = v[h * DH : (h + 1) * DH]

        def store(h, gated):
            gtc[h * DH : (h + 1) * DH, :] = gated

        for h in range(HEADS // 2):
            attend(k, qzc[h], vtc, g, hidden_rows, (2 * h, 2 * h + 1), 128, store)
        gcol[i] = transposed(gtc[...])

    @pl.loop(0, 8)
    def _(b):
        at = pl.multiple_of(b * 16, 16)
        rows = mm(swap[...], gcol[:, pl.ds(at, 16), :].reshape(256, 256)).astype(BF16)
        mid = recv_m[pl.ds(2 * b, 2)].reshape(256, 256).astype(F32)
        out_al[pl.ds(at, 16)] = (mid + mm(rows, cwo[...])).astype(BF16).reshape(16, 16, 256)

    wait_all(send_c, recv_c, s_c, r_c)

    total = jnp.zeros((16, 256), F32)
    total = lax.fori_loop(0, N, lambda d, t: t + jnp.sum(recv_c[d].astype(F32), axis=0), total)
    mean = total * (1.0 / 128)

    def spread(d, t):
        center = recv_c[d].astype(F32) - mean[None]
        return t + jnp.sum(center * center, axis=0)

    variance = lax.fori_loop(0, N, spread, jnp.zeros((16, 256), F32)) * (1.0 / 128)
    rate = lax.rsqrt(variance + EPSILON)

    @pl.loop(0, 8)
    def _(g):
        block = recv_c[pl.ds(2 * g, 2)].reshape(16, 16, 256).astype(F32)
        normed = ((block - mean[None]) * rate[None]).astype(BF16).reshape(256, 256)
        at = pl.multiple_of(g * 16, 16)
        cnt[:, pl.ds(at, 16), :] = mm(swap[...], normed).astype(BF16).reshape(16, 16, 256)

    @pl.loop(0, 16)
    def _(i):
        update = tn(cnt[i], tow[...])
        mid = (pr[i].astype(F32) + update * gate[i]).astype(BF16)
        middle = mid.astype(F32)
        hidden = jnp.maximum(mm(normalize(middle), tiw[...]), 0.0).astype(BF16)
        out_pr[i] = (middle + mm(hidden, tww[...])).astype(BF16)

    @pl.loop(1, N)
    def _(o):
        d = peer(o)
        send_bias(d).wait_send()
        send_to(send_lr, recv_lr, s_lr, r_lr, d).wait_send()
        send_to(send_m, recv_m, s_m, r_m, d).wait_send()
        send_to(send_c, recv_c, s_c, r_c, d).wait_send()


def shards(
    alignment, pair_state, residue_present_mask, alignment_row_mask,
    row_query_weight, row_key_weight, row_value_weight, row_gate_weight, row_output_weight,
    pair_bias_weight,
    column_query_weight, column_key_weight, column_value_weight, column_gate_weight, column_output_weight,
    triangle_left_weight, triangle_right_weight, triangle_gate_weight, triangle_output_weight,
    transition_input_weight, transition_output_weight,
):
    vmem = pl.BlockSpec(memory_space=pltpu.VMEM)
    smem = pl.BlockSpec(memory_space=pltpu.SMEM)
    dma = pltpu.SemaphoreType.DMA((N,))
    return tuple(
        pl.pallas_call(
            kernel,
            out_shape=(
                jax.ShapeDtypeStruct((128, 16, 256), BF16),
                jax.ShapeDtypeStruct((16, 256, 128), BF16),
            ),
            in_specs=[vmem, vmem, smem] + [vmem] * 19,
            out_specs=(vmem, vmem),
            scratch_shapes=[
                pltpu.VMEM((16, 256, 128), BF16),
                pltpu.VMEM((16, 256, 256), BF16),
                pltpu.VMEM((16, 16, 256), BF16),
                pltpu.VMEM((N, 2, 8, 16, 256), BF16),
                pltpu.VMEM((N, 2, 8, 16, 256), BF16),
                pltpu.VMEM((8, 16, 256), BF16),
                pltpu.VMEM((N, 8, 16, 256), BF16),
                pltpu.VMEM((8, 256, 256), F32),
                pltpu.VMEM((N, 8, 16, 256), BF16),
                pltpu.VMEM((N, 8, 16, 256), BF16),
                pltpu.VMEM((N, 8, 16, 256), BF16),
                pltpu.VMEM((N, 8, 16, 256), BF16),
                pltpu.VMEM((6, 256, 256), BF16),
                pltpu.VMEM((256, 128), BF16),
                pltpu.VMEM((128, 128), F32),
                pltpu.VMEM((8, 256, 256), BF16),
                pltpu.VMEM((8, 48, 256), BF16),
                pltpu.VMEM((4, 256, 256), BF16),
                pltpu.VMEM((8, 48, 128), BF16),
                pltpu.VMEM((256, 256), BF16),
                pltpu.VMEM((256, 128), BF16),
                pltpu.VMEM((16, 128, 256), BF16),
                pltpu.VMEM((16, 128, 256), BF16),
                pltpu.VMEM((16, 128, 256), BF16),
                pltpu.VMEM((16, 256, 128), F32),
                pltpu.VMEM((256, 256), BF16),
                pltpu.VMEM((256, 256), BF16),
            ]
            + [dma] * 8,
            compiler_params=pltpu.CompilerParams(
                collective_id=0, has_side_effects=True, vmem_limit_bytes=56 << 20
            ),
        )(
            alignment, pair_state, residue_present_mask,
            residue_present_mask.reshape(1, 256), alignment_row_mask.reshape(1, 128),
            row_query_weight, row_key_weight, row_value_weight, row_gate_weight, row_output_weight,
            pair_bias_weight,
            column_query_weight, column_key_weight, column_value_weight, column_gate_weight,
            column_output_weight,
            triangle_left_weight, triangle_right_weight, triangle_gate_weight, triangle_output_weight,
            transition_input_weight, transition_output_weight,
        )
    )


def solution(mesh):
    in_specs = (
        P(("dp", "dap"), None, None),
        P(("dp", "dap"), None, None),
        P("dp"),
        P("dp"),
    ) + (P(),) * 17
    out_specs = (P("dp", "dap", None), P(("dp", "dap"), None, None))
    return jax.shard_map(shards, mesh=mesh, in_specs=in_specs, out_specs=out_specs, check_vma=False)
```

```python
import functools

import jax
import jax.numpy as jnp
from jax import lax
from jax.experimental import pallas as pl
from jax.experimental.pallas import tpu as pltpu
from jax.sharding import PartitionSpec as P

MESH = pl.DeviceIdType.MESH
F32 = jnp.float32
BF16 = jnp.bfloat16
N = 16
HEADS = 8
DH = 32
EPSILON = 1e-05
MASKED = -1000000000.0


def mm(a, b):
    return jnp.dot(a, b, preferred_element_type=F32)


def nt(a, b):
    return lax.dot_general(a, b, (((1,), (1,)), ((), ())), preferred_element_type=F32)


def tn(a, b):
    return lax.dot_general(a, b, (((0,), (0,)), ((), ())), preferred_element_type=F32)


def normalize(x):
    center = x - jnp.mean(x, axis=-1, keepdims=True)
    variance = jnp.mean(center * center, axis=-1, keepdims=True)
    return (center * lax.rsqrt(variance + EPSILON)).astype(BF16)


def sigmoid(x):
    return 1.0 / (1.0 + jnp.exp(-x))


def transposed(w):
    return jnp.transpose(w.astype(F32)).astype(BF16)


def attend(scores, bias, v):
    scores = scores + bias
    top = jnp.max(scores, axis=0, keepdims=True)
    mix = mm(v, jnp.exp(scores - top).astype(BF16))
    return mix[:DH] * (1.0 / mix[DH : DH + 1])


def kernel(
    pr, rmask_s, rmask, smask, pbw, tlw, trw,
    al_h, rwq_h, rwk_h, rwv_h, rwg_h, rwo_h, cwq_h, cwk_h, cwv_h, cwg_h, cwo_h, tgw_h, tow_h, tiw_h, tww_h,
    out_al, out_pr,
    pn, lr_t, b_t, send_lr, recv_lr, recv_b, bias_t, send_m, recv_m, send_c, recv_c,
    wt, wlr, qs, kz, vt, gs, gt, st, st_c, cn, gcol, cnt, gate, swap, eye,
    al, rwq, rwk, rwv, rwg, rwo, cwq, cwk, cwv, cwg, cwo, tgw, tow, tiw, tww, al_v, pr_v,
    s_lr, r_lr, s_b, r_b, s_x, r_x, s_m, r_m, s_c, r_c, s_in, s_out,
):
    me = lax.axis_index("dap")

    def peer(o):
        return lax.rem(me + o, N)

    barrier = pltpu.get_barrier_semaphore()
    for o in range(1, N):
        pl.semaphore_signal(barrier, inc=1, device_id={"dap": peer(o)}, device_id_type=MESH)

    loads = [
        pltpu.make_async_copy(src, dst, s_in.at[n])
        for n, (src, dst) in enumerate(
            zip(
                (rwq_h, rwv_h, rwg_h, cwq_h, cwv_h, cwg_h, tgw_h, al_h, rwk_h, rwo_h, cwk_h, cwo_h, tow_h, tiw_h, tww_h),
                (rwq, rwv, rwg, cwq, cwv, cwg, tgw, al, rwk, rwo, cwk, cwo, tow, tiw, tww),
            )
        )
    ]
    for load in loads:
        load.start()

    def copy(src, dst, ssem, rsem, to):
        return pltpu.make_async_remote_copy(
            src_ref=src, dst_ref=dst, send_sem=ssem, recv_sem=rsem,
            device_id={"dap": to}, device_id_type=MESH,
        )

    def send_to(send, recv, ssem, rsem, d):
        return copy(send.at[d], recv.at[me], ssem.at[d], rsem.at[me], d)

    def arrival(send, recv, ssem, rsem, d):
        return copy(send.at[d], recv.at[d], ssem.at[d], rsem.at[d], d)

    def wait_all(send, recv, ssem, rsem):
        @pl.loop(1, N)
        def _(o):
            arrival(send, recv, ssem, rsem, peer(o)).wait_recv()

    row = lax.broadcasted_iota(jnp.int32, (256, 256), 0)
    col = lax.broadcasted_iota(jnp.int32, (256, 256), 1)
    swap[...] = jnp.where(col == (row % 16) * 16 + row // 16, 1.0, 0.0).astype(BF16)
    eye[...] = jnp.where(col == row, 1.0, 0.0).astype(BF16)

    wlr[:128, :] = transposed(tlw[...])
    wlr[128:, :] = transposed(trw[...])
    live = rmask[...].astype(F32)

    b_t[...] = jnp.zeros_like(b_t)

    @pl.loop(0, 16, unroll=4)
    def _(i):
        normed = normalize(pr[i].astype(F32))
        pn[i] = normed
        own = rmask_s[me * 16 + i].astype(F32)
        lr_t[i] = (nt(wlr[...], normed) * (live * own)).astype(BF16)
        b_t[i, :HEADS] = nt(pbw[...], normed).astype(BF16)

    recv_b[me] = mm(swap[...], b_t[...].reshape(256, 256))[:128].astype(BF16).reshape(8, 16, 256)

    pl.semaphore_wait(barrier, N - 1)

    high = me // 8
    depth = lax.rem(me, 8)

    def along(dz):
        return high * 8 + lax.rem(depth + dz + 8, 8)

    across = lax.rem(me + 8, N)

    def pass_bias(n, origin, to):
        return copy(recv_b.at[origin], recv_b.at[origin], s_b.at[n], r_b.at[origin], to)

    def pass_across(origin):
        return copy(recv_b.at[origin], recv_b.at[origin], s_x.at[origin], r_b.at[origin], across)

    first_hops = [pass_bias(n, me, along(dz)) for n, dz in enumerate((1, -1, 2, -2))]
    second_hops = [
        pass_bias(4 + n, along(at), along(to)) for n, (at, to) in enumerate(((-2, 1), (2, -1), (-2, 2)))
    ]
    for hop in first_hops:
        hop.start()
    pass_across(me).start()

    def split_group(g):
        at = pl.multiple_of(g * 16, 16)
        for side in range(2):
            block = lr_t[:, pl.ds(side * 128 + at, 16), :].reshape(256, 256)
            swapped = mm(swap[...], block).astype(BF16).reshape(2, 8, 16, 256)
            send_lr[2 * g, side] = swapped[0]
            send_lr[2 * g + 1, side] = swapped[1]

    def send_group(n):
        g = lax.rem(me // 2 + n, 8)
        split_group(g)
        send_to(send_lr, recv_lr, s_lr, r_lr, 2 * g).start()
        send_to(send_lr, recv_lr, s_lr, r_lr, 2 * g + 1).start()

    @pl.loop(1, 3)
    def _(n):
        send_group(n)

    for n, w in enumerate((rwq, rwv, rwg, cwq, cwv, cwg)):
        loads[n].wait()
        wt[n] = transposed(w[...])

    for dz in (2, -2, 1, -1):
        pass_across(along(dz)).wait_recv()
    for hop in second_hops:
        hop.start()
    for dz in (2, -2, 1, -1):
        pass_across(along(dz)).start()

    @pl.loop(3, 8)
    def _(n):
        send_group(n)

    split_group(me // 2)
    near = me + 1 - 2 * (me % 2)
    send_to(send_lr, recv_lr, s_lr, r_lr, near).start()
    recv_lr[me] = send_lr[me]

    vt[:, DH:, :] = jnp.ones((HEADS, 16, 256), BF16)

    loads[6].wait()

    @pl.loop(0, 16, unroll=4)
    def _(i):
        gate[i] = sigmoid(mm(pn[i], tgw[...]))

    for dz in (3, -3, 4):
        pass_across(along(dz)).wait_recv()
        pass_across(along(dz)).start()
    for dz in range(8):
        pass_across((1 - high) * 8 + dz).wait_recv()
    shown = nt(eye[...], jnp.broadcast_to(live, (256, 256)).astype(BF16))
    hidden_keys = (1.0 - shown) * MASKED

    @pl.loop(0, HEADS, unroll=2)
    def _(h):
        bias_t[h] = nt(eye[...], recv_b[:, h].reshape(256, 256)) + hidden_keys

    scale = DH ** (-0.5)
    for load in loads[7:]:
        load.wait()

    lane_head = lax.broadcasted_iota(jnp.int32, (256, 256), 1) // DH

    def project(normed, first, wk):
        qs[...] = (nt(wt[first], normed) * scale).astype(BF16)
        v = nt(wt[first + 1], normed).astype(BF16)
        gs[...] = sigmoid(nt(wt[first + 2], normed))
        for h in range(HEADS):
            vt[h, :DH, :] = v[h * DH : (h + 1) * DH]
        return mm(normed, wk[...])

    @pl.loop(0, 8)
    def _(s):
        k = project(normalize(al[s].astype(F32)), 0, rwk)
        for h in range(HEADS):
            kz[h * 256 : (h + 1) * 256, :] = jnp.where(lane_head == h, k, 0.0).astype(BF16)
        st[...] = mm(kz[...], qs[...])
        for h in range(HEADS):
            own = slice(h * DH, (h + 1) * DH)
            gt[own, :] = (attend(st[h * 256 : (h + 1) * 256, :], bias_t[h], vt[h]) * gs[own, :]).astype(BF16)
        mid = (al[s].astype(F32) + tn(gt[...], rwo[...])).astype(BF16)
        send_m[:, s] = mid.reshape(16, 16, 256)

    for o in range(1, N):
        send_to(send_m, recv_m, s_m, r_m, peer(o)).start()
    recv_m[me] = send_m[me]

    wait_all(send_lr, recv_lr, s_lr, r_lr)

    def send_half(n, d):
        return copy(send_c.at[n, d], recv_c.at[n, me], s_c.at[n, d], r_c.at[n, me], d)

    for n in range(2):

        @pl.loop(0, 8, unroll=2)
        def _(c):
            left = recv_lr[:, 0, c].reshape(256, 256)
            right = recv_lr[n * 8 : n * 8 + 8, 1, c].reshape(128, 256)
            send_c[n, :, c] = nt(left, right).astype(BF16).reshape(16, 16, 128)

        for o in range(1, N):
            send_half(n, peer(o)).start()
        recv_c[n, me] = send_c[n, me]

    wait_all(send_m, recv_m, s_m, r_m)

    @pl.loop(0, 8)
    def _(b):
        rows = recv_m[pl.ds(2 * b, 2)].reshape(256, 256).astype(F32)
        at = pl.multiple_of(b * 16, 16)
        cn[:, pl.ds(at, 16), :] = mm(swap[...], normalize(rows)).astype(BF16).reshape(16, 16, 256)

    seen = nt(eye[:128, :128], jnp.broadcast_to(smask[...].astype(F32), (128, 128)).astype(BF16))
    hidden_rows = (1.0 - seen) * MASKED

    @pl.loop(0, 8)
    def _(p):
        k = project(cn[pl.ds(2 * p, 2)].reshape(256, 256), 3, cwk)
        for h in range(HEADS):
            one = jnp.where(lane_head == h, k, 0.0).astype(BF16)
            kz[h * 128 : (h + 1) * 128, :] = one[:128]
            kz[1024 + h * 128 : 1024 + (h + 1) * 128, :] = one[128:]
        for n in range(2):
            half = slice(n * 128, n * 128 + 128)
            st_c[n] = mm(kz[n * 1024 : (n + 1) * 1024, :], qs[:, half])
        for n in range(2):
            half = slice(n * 128, n * 128 + 128)
            for h in range(HEADS):
                own = slice(h * DH, (h + 1) * DH)
                mixed = attend(st_c[n, h * 128 : (h + 1) * 128, :], hidden_rows, vt[h, :, half])
                gt[own, half] = (mixed * gs[own, half]).astype(BF16)
        for n in range(2):
            gcol[2 * p + n] = transposed(gt[:, n * 128 : n * 128 + 128])

    @pl.loop(0, 8)
    def _(b):
        at = pl.multiple_of(b * 16, 16)
        rows = mm(swap[...], gcol[:, pl.ds(at, 16), :].reshape(256, 256)).astype(BF16)
        mid = recv_m[pl.ds(2 * b, 2)].reshape(256, 256).astype(F32)
        al_v[pl.ds(at, 16)] = (mid + mm(rows, cwo[...])).astype(BF16).reshape(16, 16, 256)

    out_rows = pltpu.make_async_copy(al_v, out_al, s_out.at[0])
    out_rows.start()

    pair_out = [
        pltpu.make_async_copy(
            pr_v.at[:, pl.ds(n * 128, 128), :], out_pr.at[:, pl.ds(n * 128, 128), :], s_out.at[1 + n]
        )
        for n in range(2)
    ]
    for n in range(2):

        @pl.loop(1, N)
        def _(o):
            d = peer(o)
            copy(send_c.at[n, d], recv_c.at[n, d], s_c.at[n, d], r_c.at[n, d], d).wait_recv()

        def add(d, t):
            return t + jnp.sum(recv_c[n, d].astype(F32), axis=0)

        mean = lax.fori_loop(0, N, add, jnp.zeros((16, 128), F32), unroll=8) * (1.0 / 128)

        def spread(d, t):
            center = recv_c[n, d].astype(F32) - mean[None]
            return t + jnp.sum(center * center, axis=0)

        variance = lax.fori_loop(0, N, spread, jnp.zeros((16, 128), F32), unroll=8) * (1.0 / 128)
        rate = lax.rsqrt(variance + EPSILON)

        @pl.loop(0, 8, unroll=8)
        def _(g):
            block = recv_c[n, pl.ds(2 * g, 2)].reshape(16, 16, 128).astype(F32)
            normed = ((block - mean[None]) * rate[None]).astype(BF16).reshape(256, 128)
            at = pl.multiple_of(g * 16, 16)
            cnt[:, pl.ds(at, 16), :] = mm(swap[...], normed).astype(BF16).reshape(16, 16, 128)

        span = slice(n * 128, n * 128 + 128)

        @pl.loop(0, 2)
        def _(b):
            some = pl.ds(8 * b, 8)
            update = jnp.concatenate([tn(cnt[8 * b + m], tow[...]) for m in range(8)], axis=0)
            old = pr[some, span, :].reshape(1024, 128).astype(F32)
            mid = (old + update * gate[some, span, :].reshape(1024, 128)).astype(BF16)
            middle = mid.astype(F32)
            hidden = jnp.maximum(mm(normalize(middle), tiw[...]), 0.0).astype(BF16)
            pr_v[some, span, :] = (middle + mm(hidden, tww[...])).astype(BF16).reshape(8, 128, 128)

        pair_out[n].start()

    for hop in first_hops + second_hops:
        hop.wait_send()
    for dz in range(8):
        pass_across(high * 8 + dz).wait_send()

    @pl.loop(1, N)
    def _(o):
        d = peer(o)
        send_to(send_lr, recv_lr, s_lr, r_lr, d).wait_send()
        send_to(send_m, recv_m, s_m, r_m, d).wait_send()
        send_half(0, d).wait_send()
        send_half(1, d).wait_send()

    out_rows.wait()
    for done in pair_out:
        done.wait()


def shards(
    alignment, pair_state, residue_present_mask, alignment_row_mask,
    row_query_weight, row_key_weight, row_value_weight, row_gate_weight, row_output_weight,
    pair_bias_weight,
    column_query_weight, column_key_weight, column_value_weight, column_gate_weight, column_output_weight,
    triangle_left_weight, triangle_right_weight, triangle_gate_weight, triangle_output_weight,
    transition_input_weight, transition_output_weight,
):
    vmem = pl.BlockSpec(memory_space=pltpu.VMEM)
    smem = pl.BlockSpec(memory_space=pltpu.SMEM)
    hbm = pl.BlockSpec(memory_space=pl.ANY)
    dma = pltpu.SemaphoreType.DMA((N,))
    return tuple(
        pl.pallas_call(
            kernel,
            out_shape=(
                jax.ShapeDtypeStruct((128, 16, 256), BF16),
                jax.ShapeDtypeStruct((16, 256, 128), BF16),
            ),
            in_specs=[vmem, smem] + [vmem] * 5 + [hbm] * 15,
            out_specs=(hbm, hbm),
            scratch_shapes=[
                pltpu.VMEM((16, 256, 128), BF16),
                pltpu.VMEM((16, 256, 256), BF16),
                pltpu.VMEM((16, 16, 256), BF16),
                pltpu.VMEM((N, 2, 8, 16, 256), BF16),
                pltpu.VMEM((N, 2, 8, 16, 256), BF16),
                pltpu.VMEM((N, 8, 16, 256), BF16),
                pltpu.VMEM((8, 256, 256), F32),
                pltpu.VMEM((N, 8, 16, 256), BF16),
                pltpu.VMEM((N, 8, 16, 256), BF16),
                pltpu.VMEM((2, N, 8, 16, 128), BF16),
                pltpu.VMEM((2, N, 8, 16, 128), BF16),
                pltpu.VMEM((6, 256, 256), BF16),
                pltpu.VMEM((256, 128), BF16),
                pltpu.VMEM((256, 256), BF16),
                pltpu.VMEM((2048, 256), BF16),
                pltpu.VMEM((8, 48, 256), BF16),
                pltpu.VMEM((256, 256), F32),
                pltpu.VMEM((256, 256), BF16),
                pltpu.VMEM((2048, 256), F32),
                pltpu.VMEM((2, 1024, 128), F32),
                pltpu.VMEM((16, 128, 256), BF16),
                pltpu.VMEM((16, 128, 256), BF16),
                pltpu.VMEM((16, 128, 128), BF16),
                pltpu.VMEM((16, 256, 128), F32),
                pltpu.VMEM((256, 256), BF16),
                pltpu.VMEM((256, 256), BF16),
            ]
            + [pltpu.VMEM((8, 256, 256), BF16)]
            + [pltpu.VMEM((256, 256), BF16)] * 10
            + [pltpu.VMEM((128, 128), BF16)] * 2
            + [
                pltpu.VMEM((128, 512), BF16),
                pltpu.VMEM((512, 128), BF16),
                pltpu.VMEM((128, 16, 256), BF16),
                pltpu.VMEM((16, 256, 128), BF16),
            ]
            + [dma] * 8
            + [pltpu.SemaphoreType.DMA((2, N))] * 2
            + [dma, pltpu.SemaphoreType.DMA((3,))],
            compiler_params=pltpu.CompilerParams(
                collective_id=0, has_side_effects=True, vmem_limit_bytes=56 << 20
            ),
        )(
            pair_state, residue_present_mask,
            residue_present_mask.reshape(1, 256), alignment_row_mask.reshape(1, 128),
            pair_bias_weight.T, triangle_left_weight, triangle_right_weight,
            alignment,
            row_query_weight, row_key_weight, row_value_weight, row_gate_weight, row_output_weight,
            column_query_weight, column_key_weight, column_value_weight, column_gate_weight,
            column_output_weight,
            triangle_gate_weight, triangle_output_weight,
            transition_input_weight, transition_output_weight,
        )
    )


def solution(mesh):
    in_specs = (
        P(("dp", "dap"), None, None),
        P(("dp", "dap"), None, None),
        P("dp"),
        P("dp"),
    ) + (P(),) * 17
    out_specs = (P("dp", "dap", None), P(("dp", "dap"), None, None))
    return jax.shard_map(shards, mesh=mesh, in_specs=in_specs, out_specs=out_specs, check_vma=False)
```

```python
import functools

import jax
import jax.numpy as jnp
from jax import lax
from jax.experimental import pallas as pl
from jax.experimental.pallas import tpu as pltpu
from jax.sharding import PartitionSpec as P

MESH = pl.DeviceIdType.MESH
F32 = jnp.float32
BF16 = jnp.bfloat16
N = 16
AHEAD = 3
HEADS = 8
DH = 32
EPSILON = 1e-05
MASKED = -1000000000.0


def mm(a, b):
    return jnp.dot(a, b, preferred_element_type=F32)


def nt(a, b):
    return lax.dot_general(a, b, (((1,), (1,)), ((), ())), preferred_element_type=F32)


def tn(a, b):
    return lax.dot_general(a, b, (((0,), (0,)), ((), ())), preferred_element_type=F32)


def normalize(x):
    center = x - jnp.mean(x, axis=-1, keepdims=True)
    variance = jnp.mean(center * center, axis=-1, keepdims=True)
    return (center * lax.rsqrt(variance + EPSILON)).astype(BF16)


def normalize_rows(x, average):
    center = x.astype(F32) - mm(x, average)
    variance = mm((center * center).astype(BF16), average)
    return (center * lax.rsqrt(variance + EPSILON)).astype(BF16)


def sigmoid(x):
    return 1.0 / (1.0 + jnp.exp(-x))


def transposed(w):
    return jnp.transpose(w.astype(F32)).astype(BF16)


def attend(scores, bias, v):
    scores = scores + bias
    top = jnp.max(scores, axis=0, keepdims=True)
    mix = mm(v, jnp.exp(scores - top).astype(BF16))
    return mix[:DH] * (1.0 / mix[DH : DH + 1])


def kernel(
    pr, rmask_s, rmask, smask, pbw, tlw, trw,
    al_h, rwq_h, rwk_h, rwv_h, rwg_h, rwo_h, cwq_h, cwk_h, cwv_h, cwg_h, cwo_h, tgw_h, tow_h, tiw_h, tww_h,
    out_al, out_pr,
    pn, lr_t, b_t, send_lr, recv_lr, recv_b, bias_t, send_m, recv_m, send_c, recv_c,
    wt, wlr, qs, kz, vt, gs, gt, st, st_c, cn, gcol, cnt, gate, swap, eye, average,
    al, rwq, rwk, rwv, rwg, rwo, cwq, cwk, cwv, cwg, cwo, tgw, tow, tiw, tww, al_v, pr_v,
    s_lr, r_lr, s_b, r_b, s_x, s_m, r_m, s_c, r_c, s_in, s_out,
):
    me = lax.axis_index("dap")

    def peer(o):
        return lax.rem(me + o, N)

    barrier = pltpu.get_barrier_semaphore()
    for o in range(1, N):
        pl.semaphore_signal(barrier, inc=1, device_id={"dap": peer(o)}, device_id_type=MESH)

    loads = [
        pltpu.make_async_copy(src, dst, s_in.at[n])
        for n, (src, dst) in enumerate(
            zip(
                (rwq_h, rwv_h, rwg_h, cwq_h, cwv_h, cwg_h, tgw_h, al_h, rwk_h, rwo_h, cwk_h, cwo_h, tow_h, tiw_h, tww_h),
                (rwq, rwv, rwg, cwq, cwv, cwg, tgw, al, rwk, rwo, cwk, cwo, tow, tiw, tww),
            )
        )
    ]
    for load in loads:
        load.start()

    def copy(src, dst, ssem, rsem, to):
        return pltpu.make_async_remote_copy(
            src_ref=src, dst_ref=dst, send_sem=ssem, recv_sem=rsem,
            device_id={"dap": to}, device_id_type=MESH,
        )

    def send_to(send, recv, ssem, rsem, d):
        return copy(send.at[d], recv.at[me], ssem.at[d], rsem.at[me], d)

    def arrival(send, recv, ssem, rsem, d):
        return copy(send.at[d], recv.at[d], ssem.at[d], rsem.at[d], d)

    def wait_all(send, recv, ssem, rsem):
        @pl.loop(1, N)
        def _(o):
            arrival(send, recv, ssem, rsem, peer(o)).wait_recv()

    row = lax.broadcasted_iota(jnp.int32, (256, 256), 0)
    col = lax.broadcasted_iota(jnp.int32, (256, 256), 1)
    swap[...] = jnp.where(col == (row % 16) * 16 + row // 16, 1.0, 0.0).astype(BF16)
    eye[...] = jnp.where(col == row, 1.0, 0.0).astype(BF16)

    wlr[:128, :] = transposed(tlw[...])
    wlr[128:, :] = transposed(trw[...])
    live = rmask[...].astype(F32)

    b_t[...] = jnp.zeros_like(b_t)
    average[...] = jnp.full((128, 128), 1.0 / 128, BF16)
    normed_pair = normalize_rows(pr[...].reshape(4096, 128), average[...])
    pn[...] = normed_pair.reshape(16, 256, 128)
    heads = nt(pbw[...], normed_pair).astype(BF16)
    for i in range(16):
        own = rmask_s[me * 16 + i].astype(F32)
        rows = slice(i * 256, i * 256 + 256)
        lr_t[i] = (nt(wlr[...], normed_pair[rows]) * (live * own)).astype(BF16)
        b_t[i, :HEADS] = heads[:, rows]

    recv_b[me] = mm(swap[...], b_t[...].reshape(256, 256))[:128].astype(BF16).reshape(8, 16, 256)

    pl.semaphore_wait(barrier, N - 1)

    high = me // 8
    depth = lax.rem(me, 8)

    def along(dz):
        return high * 8 + lax.rem(depth + dz + 8, 8)

    across = lax.rem(me + 8, N)

    def pass_bias(n, origin, to):
        return copy(recv_b.at[origin], recv_b.at[origin], s_b.at[n], r_b.at[origin], to)

    def pass_across(origin):
        return copy(recv_b.at[origin], recv_b.at[origin], s_x.at[origin], r_b.at[origin], across)

    first_hops = [pass_bias(n, me, along(dz)) for n, dz in enumerate((1, -1, 2, -2))]
    second_hops = [
        pass_bias(4 + n, along(at), along(to)) for n, (at, to) in enumerate(((-2, 1), (2, -1), (-2, 2)))
    ]
    for hop in first_hops:
        hop.start()
    pass_across(me).start()

    def split_group(g):
        at = pl.multiple_of(g * 16, 16)
        for side in range(2):
            block = lr_t[:, pl.ds(side * 128 + at, 16), :].reshape(256, 256)
            swapped = mm(swap[...], block).astype(BF16).reshape(2, 8, 16, 256)
            send_lr[2 * g, side] = swapped[0]
            send_lr[2 * g + 1, side] = swapped[1]

    def send_group(n):
        g = lax.rem(me // 2 + n, 8)
        split_group(g)
        send_to(send_lr, recv_lr, s_lr, r_lr, 2 * g).start()
        send_to(send_lr, recv_lr, s_lr, r_lr, 2 * g + 1).start()

    @pl.loop(1, AHEAD)
    def _(n):
        send_group(n)

    for n, w in enumerate((rwq, rwv, rwg, cwq, cwv, cwg)):
        loads[n].wait()
        wt[n] = transposed(w[...])

    for dz in (2, -2, 1, -1):
        pass_across(along(dz)).wait_recv()
    for hop in second_hops:
        hop.start()
    for dz in (2, -2, 1, -1):
        pass_across(along(dz)).start()

    @pl.loop(AHEAD, 8)
    def _(n):
        send_group(n)

    split_group(me // 2)
    near = me + 1 - 2 * (me % 2)
    send_to(send_lr, recv_lr, s_lr, r_lr, near).start()
    recv_lr[me] = send_lr[me]

    vt[:, DH:, :] = jnp.ones((HEADS, 16, 256), BF16)

    loads[6].wait()

    gate[...] = sigmoid(mm(pn[...].reshape(4096, 128), tgw[...])).reshape(16, 256, 128)

    for dz in (3, -3, 4):
        pass_across(along(dz)).wait_recv()
        pass_across(along(dz)).start()
    for dz in range(8):
        pass_across((1 - high) * 8 + dz).wait_recv()
    shown = nt(eye[...], jnp.broadcast_to(live, (256, 256)).astype(BF16))
    hidden_keys = (1.0 - shown) * MASKED

    @pl.loop(0, HEADS, unroll=2)
    def _(h):
        bias_t[h] = nt(eye[...], recv_b[:, h].reshape(256, 256)) + hidden_keys

    scale = DH ** (-0.5)
    for load in loads[7:]:
        load.wait()

    lane_head = lax.broadcasted_iota(jnp.int32, (256, 256), 1) // DH

    def project(normed, first, wk):
        qs[...] = (nt(wt[first], normed) * scale).astype(BF16)
        v = nt(wt[first + 1], normed).astype(BF16)
        gs[...] = sigmoid(nt(wt[first + 2], normed))
        for h in range(HEADS):
            vt[h, :DH, :] = v[h * DH : (h + 1) * DH]
        return mm(normed, wk[...])

    def send_rows(n, d):
        some = pl.ds(4 * n, 4)
        return copy(send_m.at[d, some], recv_m.at[me, some], s_m.at[n, d], r_m.at[n, me], d)

    def row(s):
        k = project(normalize(al[s].astype(F32)), 0, rwk)
        for h in range(HEADS):
            kz[h * 256 : (h + 1) * 256, :] = jnp.where(lane_head == h, k, 0.0).astype(BF16)
        st[...] = mm(kz[...], qs[...])
        for h in range(HEADS):
            own = slice(h * DH, (h + 1) * DH)
            gt[own, :] = (attend(st[h * 256 : (h + 1) * 256, :], bias_t[h], vt[h]) * gs[own, :]).astype(BF16)
        mid = (al[s].astype(F32) + tn(gt[...], rwo[...])).astype(BF16)
        send_m[:, s] = mid.reshape(16, 16, 256)

    for n in range(2):
        pl.loop(4 * n, 4 * n + 4)(row)
        for o in range(1, N):
            send_rows(n, peer(o)).start()

    recv_m[me] = send_m[me]

    wait_all(send_lr, recv_lr, s_lr, r_lr)

    def send_half(n, d):
        return copy(send_c.at[n, d], recv_c.at[n, me], s_c.at[n, d], r_c.at[n, me], d)

    for n in range(2):

        @pl.loop(0, 8, unroll=2)
        def _(c):
            left = recv_lr[:, 0, c].reshape(256, 256)
            right = recv_lr[n * 8 : n * 8 + 8, 1, c].reshape(128, 256)
            send_c[n, :, c] = nt(left, right).astype(BF16).reshape(16, 16, 128)

        for o in range(1, N):
            send_half(n, peer(o)).start()
        recv_c[n, me] = send_c[n, me]

    @pl.loop(1, N)
    def _(o):
        d = peer(o)
        for n in range(2):
            some = pl.ds(4 * n, 4)
            copy(send_m.at[d, some], recv_m.at[d, some], s_m.at[n, d], r_m.at[n, d], d).wait_recv()


    @pl.loop(0, 8)
    def _(b):
        rows = recv_m[pl.ds(2 * b, 2)].reshape(256, 256).astype(F32)
        at = pl.multiple_of(b * 16, 16)
        cn[:, pl.ds(at, 16), :] = mm(swap[...], normalize(rows)).astype(BF16).reshape(16, 16, 256)

    seen = nt(eye[:128, :128], jnp.broadcast_to(smask[...].astype(F32), (128, 128)).astype(BF16))
    hidden_rows = (1.0 - seen) * MASKED

    @pl.loop(0, 8)
    def _(p):
        k = project(cn[pl.ds(2 * p, 2)].reshape(256, 256), 3, cwk)
        for h in range(HEADS):
            one = jnp.where(lane_head == h, k, 0.0).astype(BF16)
            kz[h * 128 : (h + 1) * 128, :] = one[:128]
            kz[1024 + h * 128 : 1024 + (h + 1) * 128, :] = one[128:]
        for n in range(2):
            half = slice(n * 128, n * 128 + 128)
            st_c[n] = mm(kz[n * 1024 : (n + 1) * 1024, :], qs[:, half])
        for n in range(2):
            half = slice(n * 128, n * 128 + 128)
            for h in range(HEADS):
                own = slice(h * DH, (h + 1) * DH)
                mixed = attend(st_c[n, h * 128 : (h + 1) * 128, :], hidden_rows, vt[h, :, half])
                gt[own, half] = (mixed * gs[own, half]).astype(BF16)
        for n in range(2):
            gcol[2 * p + n] = transposed(gt[:, n * 128 : n * 128 + 128])

    @pl.loop(0, 8)
    def _(b):
        at = pl.multiple_of(b * 16, 16)
        rows = mm(swap[...], gcol[:, pl.ds(at, 16), :].reshape(256, 256)).astype(BF16)
        mid = recv_m[pl.ds(2 * b, 2)].reshape(256, 256).astype(F32)
        al_v[pl.ds(at, 16)] = (mid + mm(rows, cwo[...])).astype(BF16).reshape(16, 16, 256)

    out_rows = pltpu.make_async_copy(al_v, out_al, s_out.at[0])
    out_rows.start()

    pair_out = [
        pltpu.make_async_copy(
            pr_v.at[:, pl.ds(n * 128, 128), :], out_pr.at[:, pl.ds(n * 128, 128), :], s_out.at[1 + n]
        )
        for n in range(2)
    ]
    for n in range(2):

        @pl.loop(1, N)
        def _(o):
            d = peer(o)
            copy(send_c.at[n, d], recv_c.at[n, d], s_c.at[n, d], r_c.at[n, d], d).wait_recv()

        def add(d, t):
            return t + jnp.sum(recv_c[n, d].astype(F32), axis=0)

        mean = lax.fori_loop(0, N, add, jnp.zeros((16, 128), F32), unroll=8) * (1.0 / 128)

        def spread(d, t):
            center = recv_c[n, d].astype(F32) - mean[None]
            return t + jnp.sum(center * center, axis=0)

        variance = lax.fori_loop(0, N, spread, jnp.zeros((16, 128), F32), unroll=8) * (1.0 / 128)
        rate = lax.rsqrt(variance + EPSILON)

        @pl.loop(0, 8, unroll=8)
        def _(g):
            block = recv_c[n, pl.ds(2 * g, 2)].reshape(16, 16, 128).astype(F32)
            normed = ((block - mean[None]) * rate[None]).astype(BF16).reshape(256, 128)
            at = pl.multiple_of(g * 16, 16)
            cnt[:, pl.ds(at, 16), :] = mm(swap[...], normed).astype(BF16).reshape(16, 16, 128)

        span = slice(n * 128, n * 128 + 128)

        update = jnp.concatenate([tn(cnt[i], tow[...]) for i in range(16)], axis=0)
        old = pr[:, span, :].reshape(2048, 128).astype(F32)
        mid = (old + update * gate[:, span, :].reshape(2048, 128)).astype(BF16)
        hidden = jnp.maximum(mm(normalize_rows(mid, average[...]), tiw[...]), 0.0).astype(BF16)
        pr_v[:, span, :] = (mid.astype(F32) + mm(hidden, tww[...])).astype(BF16).reshape(16, 128, 128)

        pair_out[n].start()

    for hop in first_hops + second_hops:
        hop.wait_send()
    for dz in range(8):
        pass_across(high * 8 + dz).wait_send()

    @pl.loop(1, N)
    def _(o):
        d = peer(o)
        send_to(send_lr, recv_lr, s_lr, r_lr, d).wait_send()
        send_rows(0, d).wait_send()
        send_rows(1, d).wait_send()
        send_half(0, d).wait_send()
        send_half(1, d).wait_send()

    out_rows.wait()
    for done in pair_out:
        done.wait()


def shards(
    alignment, pair_state, residue_present_mask, alignment_row_mask,
    row_query_weight, row_key_weight, row_value_weight, row_gate_weight, row_output_weight,
    pair_bias_weight,
    column_query_weight, column_key_weight, column_value_weight, column_gate_weight, column_output_weight,
    triangle_left_weight, triangle_right_weight, triangle_gate_weight, triangle_output_weight,
    transition_input_weight, transition_output_weight,
):
    vmem = pl.BlockSpec(memory_space=pltpu.VMEM)
    smem = pl.BlockSpec(memory_space=pltpu.SMEM)
    hbm = pl.BlockSpec(memory_space=pl.ANY)
    dma = pltpu.SemaphoreType.DMA((N,))
    return tuple(
        pl.pallas_call(
            kernel,
            out_shape=(
                jax.ShapeDtypeStruct((128, 16, 256), BF16),
                jax.ShapeDtypeStruct((16, 256, 128), BF16),
            ),
            in_specs=[vmem, smem] + [vmem] * 5 + [hbm] * 15,
            out_specs=(hbm, hbm),
            scratch_shapes=[
                pltpu.VMEM((16, 256, 128), BF16),
                pltpu.VMEM((16, 256, 256), BF16),
                pltpu.VMEM((16, 16, 256), BF16),
                pltpu.VMEM((N, 2, 8, 16, 256), BF16),
                pltpu.VMEM((N, 2, 8, 16, 256), BF16),
                pltpu.VMEM((N, 8, 16, 256), BF16),
                pltpu.VMEM((8, 256, 256), F32),
                pltpu.VMEM((N, 8, 16, 256), BF16),
                pltpu.VMEM((N, 8, 16, 256), BF16),
                pltpu.VMEM((2, N, 8, 16, 128), BF16),
                pltpu.VMEM((2, N, 8, 16, 128), BF16),
                pltpu.VMEM((6, 256, 256), BF16),
                pltpu.VMEM((256, 128), BF16),
                pltpu.VMEM((256, 256), BF16),
                pltpu.VMEM((2048, 256), BF16),
                pltpu.VMEM((8, 48, 256), BF16),
                pltpu.VMEM((256, 256), F32),
                pltpu.VMEM((256, 256), BF16),
                pltpu.VMEM((2048, 256), F32),
                pltpu.VMEM((2, 1024, 128), F32),
                pltpu.VMEM((16, 128, 256), BF16),
                pltpu.VMEM((16, 128, 256), BF16),
                pltpu.VMEM((16, 128, 128), BF16),
                pltpu.VMEM((16, 256, 128), F32),
                pltpu.VMEM((256, 256), BF16),
                pltpu.VMEM((256, 256), BF16),
                pltpu.VMEM((128, 128), BF16),
            ]
            + [pltpu.VMEM((8, 256, 256), BF16)]
            + [pltpu.VMEM((256, 256), BF16)] * 10
            + [pltpu.VMEM((128, 128), BF16)] * 2
            + [
                pltpu.VMEM((128, 512), BF16),
                pltpu.VMEM((512, 128), BF16),
                pltpu.VMEM((128, 16, 256), BF16),
                pltpu.VMEM((16, 256, 128), BF16),
            ]
            + [dma] * 5
            + [pltpu.SemaphoreType.DMA((2, N))] * 4
            + [dma, pltpu.SemaphoreType.DMA((3,))],
            compiler_params=pltpu.CompilerParams(
                collective_id=0, has_side_effects=True, vmem_limit_bytes=56 << 20
            ),
        )(
            pair_state, residue_present_mask,
            residue_present_mask.reshape(1, 256), alignment_row_mask.reshape(1, 128),
            pair_bias_weight.T, triangle_left_weight, triangle_right_weight,
            alignment,
            row_query_weight, row_key_weight, row_value_weight, row_gate_weight, row_output_weight,
            column_query_weight, column_key_weight, column_value_weight, column_gate_weight,
            column_output_weight,
            triangle_gate_weight, triangle_output_weight,
            transition_input_weight, transition_output_weight,
        )
    )


def solution(mesh):
    in_specs = (
        P(("dp", "dap"), None, None),
        P(("dp", "dap"), None, None),
        P("dp"),
        P("dp"),
    ) + (P(),) * 17
    out_specs = (P("dp", "dap", None), P(("dp", "dap"), None, None))
    return jax.shard_map(shards, mesh=mesh, in_specs=in_specs, out_specs=out_specs, check_vma=False)
```

```python
import functools

import jax
import jax.numpy as jnp
from jax import lax
from jax.experimental import pallas as pl
from jax.experimental.pallas import tpu as pltpu
from jax.sharding import PartitionSpec as P

MESH = pl.DeviceIdType.MESH
F32 = jnp.float32
BF16 = jnp.bfloat16
N = 16
AHEAD = 3
HEADS = 8
DH = 32
EPSILON = 1e-05
MASKED = -1000000000.0


def mm(a, b):
    return jnp.dot(a, b, preferred_element_type=F32)


def nt(a, b):
    return lax.dot_general(a, b, (((1,), (1,)), ((), ())), preferred_element_type=F32)


def tn(a, b):
    return lax.dot_general(a, b, (((0,), (0,)), ((), ())), preferred_element_type=F32)


def normalize(x):
    center = x - jnp.mean(x, axis=-1, keepdims=True)
    variance = jnp.mean(center * center, axis=-1, keepdims=True)
    return (center * lax.rsqrt(variance + EPSILON)).astype(BF16)


def normalize_rows(x, average):
    center = x.astype(F32) - mm(x, average)
    variance = mm((center * center).astype(BF16), average)
    return (center * lax.rsqrt(variance + EPSILON)).astype(BF16)


def sigmoid(x):
    return 1.0 / (1.0 + jnp.exp(-x))


def transposed(w):
    return jnp.transpose(w.astype(F32)).astype(BF16)


def attend(scores, bias, v):
    scores = scores + bias
    top = jnp.max(scores, axis=0, keepdims=True)
    mix = mm(v, jnp.exp(scores - top).astype(BF16))
    return mix[:DH] * (1.0 / mix[DH : DH + 1])


def finish(received, rest, cnt, swap, average, tow, tiw, tww):
    def add(d, t):
        return t + jnp.sum(received[d].astype(F32), axis=0)

    mean = lax.fori_loop(0, N, add, jnp.zeros((16, 128), F32), unroll=8) * (1.0 / 128)

    def spread(d, t):
        center = received[d].astype(F32) - mean[None]
        return t + jnp.sum(center * center, axis=0)

    variance = lax.fori_loop(0, N, spread, jnp.zeros((16, 128), F32), unroll=8) * (1.0 / 128)
    rate = lax.rsqrt(variance + EPSILON)

    @pl.loop(0, 8, unroll=8)
    def _(g):
        block = received[pl.ds(2 * g, 2)].reshape(16, 16, 128).astype(F32)
        normed = ((block - mean[None]) * rate[None]).astype(BF16).reshape(256, 128)
        at = pl.multiple_of(g * 16, 16)
        cnt[:, pl.ds(at, 16), :] = mm(swap, normed).astype(BF16).reshape(16, 16, 128)

    old, gates = rest()
    update = jnp.concatenate([tn(cnt[i], tow[...]) for i in range(16)], axis=0)
    mid = (old.reshape(2048, 128).astype(F32) + update * gates.reshape(2048, 128)).astype(BF16)
    hidden = jnp.maximum(mm(normalize_rows(mid, average), tiw[...]), 0.0).astype(BF16)
    return (mid.astype(F32) + mm(hidden, tww[...])).astype(BF16).reshape(16, 128, 128)


def constants():
    row = lax.broadcasted_iota(jnp.int32, (256, 256), 0)
    col = lax.broadcasted_iota(jnp.int32, (256, 256), 1)
    swap = jnp.where(col == (row % 16) * 16 + row // 16, 1.0, 0.0).astype(BF16)
    eye = jnp.where(col == row, 1.0, 0.0).astype(BF16)
    return swap, eye, jnp.full((128, 128), 1.0 / 128, BF16)


def last_half(
    al_h, first_h, received_h, gate_h, pr_h, tow_h, tiw_h, tww_h, out_al, out_pr,
    al, first, received, gate, old, tow, tiw, tww, cnt, done, s_in, s_out,
):
    half = pl.ds(128, 128)
    loads = [
        pltpu.make_async_copy(src, dst, s_in.at[n])
        for n, (src, dst) in enumerate(
            (
                (received_h, received), (tow_h, tow), (pr_h.at[:, half, :], old), (gate_h, gate),
                (tiw_h, tiw), (tww_h, tww), (al_h, al), (first_h, first),
            )
        )
    ]
    for load in loads:
        load.start()
    swap, _, average = constants()
    loads[0].wait()
    stores = [
        pltpu.make_async_copy(al, out_al, s_out.at[0]),
        pltpu.make_async_copy(first, out_pr.at[:, pl.ds(0, 128), :], s_out.at[1]),
        pltpu.make_async_copy(done, out_pr.at[:, half, :], s_out.at[2]),
    ]

    def rest():
        for load in loads[1:]:
            load.wait()
        stores[0].start()
        stores[1].start()
        return old[...], gate[...]

    done[...] = finish(received, rest, cnt, swap, average, tow, tiw, tww)
    stores[2].start()
    for store in stores:
        store.wait()


def kernel(
    pr_h, rmask_s_h, rmask_h, smask_h, pbw_h, tlw_h, trw_h, al_h, rwq_h, rwk_h, rwv_h, rwg_h, rwo_h, cwq_h, cwk_h, cwv_h, cwg_h, cwo_h, tgw_h, tow_h, tiw_h, tww_h,
    out_al, out_pr, out_c, out_gate,
    pn, lr_t, b_t, send_lr, recv_lr, recv_b, bias_t, send_m, recv_m, send_c, recv_c,
    wt, wlr, qs, kz, vt, gs, gt, st, st_c, cn, gcol, cnt, gate, swap, eye, average,
    al, rwq, rwk, rwv, rwg, rwo, cwq, cwk, cwv, cwg, cwo, tgw, tow, tiw, tww, al_v, pr_v, pr, rmask_s, rmask, smask, pbw, tlw, trw,
    s_lr, r_lr, s_b, r_b, s_x, s_m, r_m, s_c, r_c, s_in, s_out, s_first,
):
    me = lax.axis_index("dap")

    def peer(o):
        return lax.rem(me + o, N)

    barrier = pltpu.get_barrier_semaphore()
    for o in range(1, N):
        pl.semaphore_signal(barrier, inc=1, device_id={"dap": peer(o)}, device_id_type=MESH)

    first_loads = [
        pltpu.make_async_copy(src, dst, s_first.at[n])
        for n, (src, dst) in enumerate(
            zip(
                (pr_h, tlw_h, trw_h, rmask_s_h, rmask_h, pbw_h, smask_h),
                (pr, tlw, trw, rmask_s, rmask, pbw, smask),
            )
        )
    ]
    loads = [
        pltpu.make_async_copy(src, dst, s_in.at[n])
        for n, (src, dst) in enumerate(
            zip(
                (rwq_h, rwv_h, rwg_h, cwq_h, cwv_h, cwg_h, tgw_h, al_h, rwk_h, rwo_h, cwk_h, cwo_h, tow_h, tiw_h, tww_h),
                (rwq, rwv, rwg, cwq, cwv, cwg, tgw, al, rwk, rwo, cwk, cwo, tow, tiw, tww),
            )
        )
    ]
    for load in first_loads:
        load.start()

    def copy(src, dst, ssem, rsem, to):
        return pltpu.make_async_remote_copy(
            src_ref=src, dst_ref=dst, send_sem=ssem, recv_sem=rsem,
            device_id={"dap": to}, device_id_type=MESH,
        )

    def send_to(send, recv, ssem, rsem, d):
        return copy(send.at[d], recv.at[me], ssem.at[d], rsem.at[me], d)

    def arrival(send, recv, ssem, rsem, d):
        return copy(send.at[d], recv.at[d], ssem.at[d], rsem.at[d], d)

    def wait_all(send, recv, ssem, rsem):
        @pl.loop(1, N)
        def _(o):
            arrival(send, recv, ssem, rsem, peer(o)).wait_recv()

    swap[...], eye[...], average[...] = constants()

    for load in first_loads:
        load.wait()
    for load in loads:
        load.start()
    wlr[:128, :] = transposed(tlw[...])
    wlr[128:, :] = transposed(trw[...])
    live = rmask[...].astype(F32)

    b_t[...] = jnp.zeros_like(b_t)
    normed_pair = normalize_rows(pr[...].reshape(4096, 128), average[...])
    pn[...] = normed_pair.reshape(16, 256, 128)
    heads = nt(pbw[...], normed_pair).astype(BF16)
    for i in range(16):
        own = rmask_s[me * 16 + i].astype(F32)
        rows = slice(i * 256, i * 256 + 256)
        lr_t[i] = (nt(wlr[...], normed_pair[rows]) * (live * own)).astype(BF16)
        b_t[i, :HEADS] = heads[:, rows]

    recv_b[me] = mm(swap[...], b_t[...].reshape(256, 256))[:128].astype(BF16).reshape(8, 16, 256)

    pl.semaphore_wait(barrier, N - 1)

    high = me // 8
    depth = lax.rem(me, 8)

    def along(dz):
        return high * 8 + lax.rem(depth + dz + 8, 8)

    across = lax.rem(me + 8, N)

    def pass_bias(n, origin, to):
        return copy(recv_b.at[origin], recv_b.at[origin], s_b.at[n], r_b.at[origin], to)

    def pass_across(origin):
        return copy(recv_b.at[origin], recv_b.at[origin], s_x.at[origin], r_b.at[origin], across)

    first_hops = [pass_bias(n, me, along(dz)) for n, dz in enumerate((1, -1, 2, -2))]
    second_hops = [
        pass_bias(4 + n, along(at), along(to)) for n, (at, to) in enumerate(((-2, 1), (2, -1), (-2, 2)))
    ]
    for hop in first_hops:
        hop.start()
    pass_across(me).start()

    def split_group(g):
        at = pl.multiple_of(g * 16, 16)
        for side in range(2):
            block = lr_t[:, pl.ds(side * 128 + at, 16), :].reshape(256, 256)
            swapped = mm(swap[...], block).astype(BF16).reshape(2, 8, 16, 256)
            send_lr[2 * g, side] = swapped[0]
            send_lr[2 * g + 1, side] = swapped[1]

    def send_group(n):
        g = lax.rem(me // 2 + n, 8)
        split_group(g)
        send_to(send_lr, recv_lr, s_lr, r_lr, 2 * g).start()
        send_to(send_lr, recv_lr, s_lr, r_lr, 2 * g + 1).start()

    @pl.loop(1, AHEAD)
    def _(n):
        send_group(n)

    for n, w in enumerate((rwq, rwv, rwg, cwq, cwv, cwg)):
        loads[n].wait()
        wt[n] = transposed(w[...])

    for dz in (2, -2, 1, -1):
        pass_across(along(dz)).wait_recv()
    for hop in second_hops:
        hop.start()
    for dz in (2, -2, 1, -1):
        pass_across(along(dz)).start()

    @pl.loop(AHEAD, 8)
    def _(n):
        send_group(n)

    split_group(me // 2)
    near = me + 1 - 2 * (me % 2)
    send_to(send_lr, recv_lr, s_lr, r_lr, near).start()
    recv_lr[me] = send_lr[me]

    vt[:, DH:, :] = jnp.ones((HEADS, 16, 256), BF16)

    loads[6].wait()

    gate[...] = sigmoid(mm(pn[...].reshape(4096, 128), tgw[...])).reshape(16, 256, 128)
    gate_out = pltpu.make_async_copy(gate.at[:, pl.ds(128, 128), :], out_gate, s_out.at[3])
    gate_out.start()

    for dz in (3, -3, 4):
        pass_across(along(dz)).wait_recv()
        pass_across(along(dz)).start()
    for dz in range(8):
        pass_across((1 - high) * 8 + dz).wait_recv()
    shown = nt(eye[...], jnp.broadcast_to(live, (256, 256)).astype(BF16))
    hidden_keys = (1.0 - shown) * MASKED

    @pl.loop(0, HEADS, unroll=2)
    def _(h):
        bias_t[h] = nt(eye[...], recv_b[:, h].reshape(256, 256)) + hidden_keys

    scale = DH ** (-0.5)
    for load in loads[7:]:
        load.wait()

    lane_head = lax.broadcasted_iota(jnp.int32, (256, 256), 1) // DH

    def project(normed, first, wk):
        qs[...] = (nt(wt[first], normed) * scale).astype(BF16)
        v = nt(wt[first + 1], normed).astype(BF16)
        gs[...] = sigmoid(nt(wt[first + 2], normed))
        for h in range(HEADS):
            vt[h, :DH, :] = v[h * DH : (h + 1) * DH]
        return mm(normed, wk[...])

    def send_rows(n, d):
        some = pl.ds(4 * n, 4)
        return copy(send_m.at[d, some], recv_m.at[me, some], s_m.at[n, d], r_m.at[n, me], d)

    def row(s):
        k = project(normalize(al[s].astype(F32)), 0, rwk)
        for h in range(HEADS):
            kz[h * 256 : (h + 1) * 256, :] = jnp.where(lane_head == h, k, 0.0).astype(BF16)
        st[...] = mm(kz[...], qs[...])
        for h in range(HEADS):
            own = slice(h * DH, (h + 1) * DH)
            gt[own, :] = (attend(st[h * 256 : (h + 1) * 256, :], bias_t[h], vt[h]) * gs[own, :]).astype(BF16)
        mid = (al[s].astype(F32) + tn(gt[...], rwo[...])).astype(BF16)
        send_m[:, s] = mid.reshape(16, 16, 256)

    for n in range(2):
        pl.loop(4 * n, 4 * n + 4)(row)
        for o in range(1, N):
            send_rows(n, peer(o)).start()

    recv_m[me] = send_m[me]

    wait_all(send_lr, recv_lr, s_lr, r_lr)

    def send_half(n, d):
        return copy(send_c.at[n, d], (recv_c, out_c)[n].at[me], s_c.at[n, d], r_c.at[n, me], d)

    for n in range(2):

        @pl.loop(0, 8, unroll=2)
        def _(c):
            left = recv_lr[:, 0, c].reshape(256, 256)
            right = recv_lr[n * 8 : n * 8 + 8, 1, c].reshape(128, 256)
            send_c[n, :, c] = nt(left, right).astype(BF16).reshape(16, 16, 128)

        for o in range(1, N):
            send_half(n, peer(o)).start()

    recv_c[me] = send_c[0, me]
    own_c = pltpu.make_async_copy(send_c.at[1, me], out_c.at[me], s_out.at[2])
    own_c.start()

    @pl.loop(1, N)
    def _(o):
        d = peer(o)
        for n in range(2):
            some = pl.ds(4 * n, 4)
            copy(send_m.at[d, some], recv_m.at[d, some], s_m.at[n, d], r_m.at[n, d], d).wait_recv()


    @pl.loop(0, 8)
    def _(b):
        rows = recv_m[pl.ds(2 * b, 2)].reshape(256, 256).astype(F32)
        at = pl.multiple_of(b * 16, 16)
        cn[:, pl.ds(at, 16), :] = mm(swap[...], normalize(rows)).astype(BF16).reshape(16, 16, 256)

    seen = nt(eye[:128, :128], jnp.broadcast_to(smask[...].astype(F32), (128, 128)).astype(BF16))
    hidden_rows = (1.0 - seen) * MASKED

    @pl.loop(0, 8)
    def _(p):
        k = project(cn[pl.ds(2 * p, 2)].reshape(256, 256), 3, cwk)
        for h in range(HEADS):
            one = jnp.where(lane_head == h, k, 0.0).astype(BF16)
            kz[h * 128 : (h + 1) * 128, :] = one[:128]
            kz[1024 + h * 128 : 1024 + (h + 1) * 128, :] = one[128:]
        for n in range(2):
            half = slice(n * 128, n * 128 + 128)
            st_c[n] = mm(kz[n * 1024 : (n + 1) * 1024, :], qs[:, half])
        for n in range(2):
            half = slice(n * 128, n * 128 + 128)
            for h in range(HEADS):
                own = slice(h * DH, (h + 1) * DH)
                mixed = attend(st_c[n, h * 128 : (h + 1) * 128, :], hidden_rows, vt[h, :, half])
                gt[own, half] = (mixed * gs[own, half]).astype(BF16)
        for n in range(2):
            gcol[2 * p + n] = transposed(gt[:, n * 128 : n * 128 + 128])

    @pl.loop(0, 8)
    def _(b):
        at = pl.multiple_of(b * 16, 16)
        rows = mm(swap[...], gcol[:, pl.ds(at, 16), :].reshape(256, 256)).astype(BF16)
        mid = recv_m[pl.ds(2 * b, 2)].reshape(256, 256).astype(F32)
        al_v[pl.ds(at, 16)] = (mid + mm(rows, cwo[...])).astype(BF16).reshape(16, 16, 256)

    out_rows = pltpu.make_async_copy(al_v, out_al, s_out.at[0])
    out_rows.start()

    def wait_half(n):
        @pl.loop(1, N)
        def _(o):
            d = peer(o)
            copy(send_c.at[n, d], (recv_c, out_c)[n].at[d], s_c.at[n, d], r_c.at[n, d], d).wait_recv()

    wait_half(0)
    pr_v[...] = finish(recv_c, lambda: (pr[:, :128, :], gate[:, :128, :]), cnt, swap[...], average[...], tow, tiw, tww)
    pair_out = pltpu.make_async_copy(pr_v, out_pr, s_out.at[1])
    pair_out.start()
    wait_half(1)

    for hop in first_hops + second_hops:
        hop.wait_send()
    for dz in range(8):
        pass_across(high * 8 + dz).wait_send()

    @pl.loop(1, N)
    def _(o):
        d = peer(o)
        send_to(send_lr, recv_lr, s_lr, r_lr, d).wait_send()
        send_rows(0, d).wait_send()
        send_rows(1, d).wait_send()
        send_half(0, d).wait_send()
        send_half(1, d).wait_send()

    for done in (out_rows, pair_out, own_c, gate_out):
        done.wait()


def shards(
    alignment, pair_state, residue_present_mask, alignment_row_mask,
    row_query_weight, row_key_weight, row_value_weight, row_gate_weight, row_output_weight,
    pair_bias_weight,
    column_query_weight, column_key_weight, column_value_weight, column_gate_weight, column_output_weight,
    triangle_left_weight, triangle_right_weight, triangle_gate_weight, triangle_output_weight,
    transition_input_weight, transition_output_weight,
):
    hbm = pl.BlockSpec(memory_space=pl.ANY)
    dma = pltpu.SemaphoreType.DMA((N,))
    al_done, pr_first, received, gates = (
        pl.pallas_call(
            kernel,
            out_shape=(
                jax.ShapeDtypeStruct((128, 16, 256), BF16),
                jax.ShapeDtypeStruct((16, 128, 128), BF16),
                jax.ShapeDtypeStruct((N, 8, 16, 128), BF16),
                jax.ShapeDtypeStruct((16, 128, 128), F32),
            ),
            in_specs=[hbm] * 22,
            out_specs=(hbm,) * 4,
            scratch_shapes=[
                pltpu.VMEM((16, 256, 128), BF16),
                pltpu.VMEM((16, 256, 256), BF16),
                pltpu.VMEM((16, 16, 256), BF16),
                pltpu.VMEM((N, 2, 8, 16, 256), BF16),
                pltpu.VMEM((N, 2, 8, 16, 256), BF16),
                pltpu.VMEM((N, 8, 16, 256), BF16),
                pltpu.VMEM((8, 256, 256), F32),
                pltpu.VMEM((N, 8, 16, 256), BF16),
                pltpu.VMEM((N, 8, 16, 256), BF16),
                pltpu.VMEM((2, N, 8, 16, 128), BF16),
                pltpu.VMEM((N, 8, 16, 128), BF16),
                pltpu.VMEM((6, 256, 256), BF16),
                pltpu.VMEM((256, 128), BF16),
                pltpu.VMEM((256, 256), BF16),
                pltpu.VMEM((2048, 256), BF16),
                pltpu.VMEM((8, 48, 256), BF16),
                pltpu.VMEM((256, 256), F32),
                pltpu.VMEM((256, 256), BF16),
                pltpu.VMEM((2048, 256), F32),
                pltpu.VMEM((2, 1024, 128), F32),
                pltpu.VMEM((16, 128, 256), BF16),
                pltpu.VMEM((16, 128, 256), BF16),
                pltpu.VMEM((16, 128, 128), BF16),
                pltpu.VMEM((16, 256, 128), F32),
                pltpu.VMEM((256, 256), BF16),
                pltpu.VMEM((256, 256), BF16),
                pltpu.VMEM((128, 128), BF16),
            ]
            + [pltpu.VMEM((8, 256, 256), BF16)]
            + [pltpu.VMEM((256, 256), BF16)] * 10
            + [pltpu.VMEM((128, 128), BF16)] * 2
            + [
                pltpu.VMEM((128, 512), BF16),
                pltpu.VMEM((512, 128), BF16),
                pltpu.VMEM((128, 16, 256), BF16),
                pltpu.VMEM((16, 128, 128), BF16),
                pltpu.VMEM((16, 256, 128), BF16),
                pltpu.SMEM((256,), jnp.int32),
                pltpu.VMEM((1, 256), jnp.int32),
                pltpu.VMEM((1, 128), jnp.int32),
                pltpu.VMEM((8, 128), BF16),
                pltpu.VMEM((128, 128), BF16),
                pltpu.VMEM((128, 128), BF16),
            ]
            + [dma] * 5
            + [pltpu.SemaphoreType.DMA((2, N))] * 4
            + [dma, pltpu.SemaphoreType.DMA((4,)), pltpu.SemaphoreType.DMA((7,))],
            compiler_params=pltpu.CompilerParams(
                collective_id=0, has_side_effects=True, vmem_limit_bytes=56 << 20
            ),
        )(
            pair_state, residue_present_mask,
            residue_present_mask.reshape(1, 256), alignment_row_mask.reshape(1, 128),
            pair_bias_weight.T, triangle_left_weight, triangle_right_weight,
            alignment,
            row_query_weight, row_key_weight, row_value_weight, row_gate_weight, row_output_weight,
            column_query_weight, column_key_weight, column_value_weight, column_gate_weight,
            column_output_weight,
            triangle_gate_weight, triangle_output_weight,
            transition_input_weight, transition_output_weight,
        )
    )
    return tuple(
        pl.pallas_call(
            last_half,
            out_shape=(
                jax.ShapeDtypeStruct((128, 16, 256), BF16),
                jax.ShapeDtypeStruct((16, 256, 128), BF16),
            ),
            in_specs=[hbm] * 8,
            out_specs=(hbm, hbm),
            scratch_shapes=[
                pltpu.VMEM((128, 16, 256), BF16),
                pltpu.VMEM((16, 128, 128), BF16),
                pltpu.VMEM((N, 8, 16, 128), BF16),
                pltpu.VMEM((16, 128, 128), F32),
                pltpu.VMEM((16, 128, 128), BF16),
                pltpu.VMEM((128, 128), BF16),
                pltpu.VMEM((128, 512), BF16),
                pltpu.VMEM((512, 128), BF16),
                pltpu.VMEM((16, 128, 128), BF16),
                pltpu.VMEM((16, 128, 128), BF16),
                pltpu.SemaphoreType.DMA((8,)),
                pltpu.SemaphoreType.DMA((3,)),
            ],
            compiler_params=pltpu.CompilerParams(vmem_limit_bytes=56 << 20),
        )(
            al_done, pr_first, received, gates, pair_state,
            triangle_output_weight, transition_input_weight, transition_output_weight,
        )
    )


def solution(mesh):
    in_specs = (
        P(("dp", "dap"), None, None),
        P(("dp", "dap"), None, None),
        P("dp"),
        P("dp"),
    ) + (P(),) * 17
    out_specs = (P("dp", "dap", None), P(("dp", "dap"), None, None))
    return jax.shard_map(shards, mesh=mesh, in_specs=in_specs, out_specs=out_specs, check_vma=False)
```

```python
import functools

import jax
import jax.numpy as jnp
from jax import lax
from jax.experimental import pallas as pl
from jax.experimental.pallas import tpu as pltpu
from jax.sharding import PartitionSpec as P

MESH = pl.DeviceIdType.MESH
F32 = jnp.float32
BF16 = jnp.bfloat16
N = 16
AHEAD = 3
HEADS = 8
DH = 32
EPSILON = 1e-05
MASKED = -1000000000.0


def mm(a, b):
    return jnp.dot(a, b, preferred_element_type=F32)


def nt(a, b):
    return lax.dot_general(a, b, (((1,), (1,)), ((), ())), preferred_element_type=F32)


def tn(a, b):
    return lax.dot_general(a, b, (((0,), (0,)), ((), ())), preferred_element_type=F32)


def normalize(x):
    center = x - jnp.mean(x, axis=-1, keepdims=True)
    variance = jnp.mean(center * center, axis=-1, keepdims=True)
    return (center * lax.rsqrt(variance + EPSILON)).astype(BF16)


def normalize_rows(x, average):
    center = x.astype(F32) - mm(x, average)
    variance = mm((center * center).astype(BF16), average)
    return (center * lax.rsqrt(variance + EPSILON)).astype(BF16)


def sigmoid(x):
    return 1.0 / (1.0 + jnp.exp(-x))


def transposed(w):
    return jnp.transpose(w.astype(F32)).astype(BF16)


def attend(scores, bias, v):
    scores = scores + bias
    top = jnp.max(scores, axis=0, keepdims=True)
    mix = mm(v, jnp.exp(scores - top).astype(BF16))
    return mix[:DH] * (1.0 / mix[DH : DH + 1])


def finish(received, rest, cnt, swap, average, tow, tiw, tww, rows):
    def both(t):
        if rows == 16:
            return t
        t = t[:8] + t[8:]
        return jnp.concatenate([t, t], axis=0)

    def add(d, t):
        return t + jnp.sum(received[d].astype(F32), axis=0)

    mean = both(lax.fori_loop(0, N, add, jnp.zeros((16, 128), F32), unroll=8)) * (1.0 / 128)

    def spread(d, t):
        center = received[d].astype(F32) - mean[None]
        return t + jnp.sum(center * center, axis=0)

    variance = both(lax.fori_loop(0, N, spread, jnp.zeros((16, 128), F32), unroll=8)) * (1.0 / 128)
    rate = lax.rsqrt(variance + EPSILON)
    channels = 256 // rows
    senders = channels // 8

    @pl.loop(0, 128 // channels, unroll=True)
    def _(g):
        block = received[pl.ds(senders * g, senders)].reshape(16, 16, 128).astype(F32)
        normed = ((block - mean[None]) * rate[None]).astype(BF16).reshape(256, 128)
        at = pl.multiple_of(g * channels, channels)
        cnt[:rows, pl.ds(at, channels), :] = mm(swap, normed).astype(BF16).reshape(rows, channels, 128)

    old, gates = rest()
    update = jnp.concatenate([tn(cnt[i], tow[...]) for i in range(rows)], axis=0)
    mid = (old.reshape(rows * 128, 128).astype(F32) + update * gates.reshape(rows * 128, 128)).astype(BF16)
    hidden = jnp.maximum(mm(normalize_rows(mid, average), tiw[...]), 0.0).astype(BF16)
    return (mid.astype(F32) + mm(hidden, tww[...])).astype(BF16).reshape(rows, 128, 128)


def constants():
    row = lax.broadcasted_iota(jnp.int32, (256, 256), 0)
    col = lax.broadcasted_iota(jnp.int32, (256, 256), 1)
    swap = jnp.where(col == (row % 16) * 16 + row // 16, 1.0, 0.0).astype(BF16)
    eye = jnp.where(col == row, 1.0, 0.0).astype(BF16)
    swap_8 = jnp.where(col == (row % 32) * 8 + row // 32, 1.0, 0.0).astype(BF16)
    return swap, swap_8, eye, jnp.full((128, 128), 1.0 / 128, BF16)


def last_part(
    al_h, first_h, second_h, received_h, gate_h, pr_h, tow_h, tiw_h, tww_h, out_al, out_pr,
    al, first, second, received, gate, old, tow, tiw, tww, cnt, done, s_in, s_out,
):
    low, high = pl.ds(0, 8), pl.ds(8, 8)
    half = pl.ds(128, 128)
    loads = [
        pltpu.make_async_copy(src, dst, s_in.at[n])
        for n, (src, dst) in enumerate(
            (
                (received_h, received), (tow_h, tow), (pr_h.at[high, half, :], old), (gate_h, gate),
                (tiw_h, tiw), (tww_h, tww), (al_h, al), (first_h, first), (second_h, second),
            )
        )
    ]
    for load in loads:
        load.start()
    _, swap_8, _, average = constants()
    stores = [
        pltpu.make_async_copy(src, dst, s_out.at[n])
        for n, (src, dst) in enumerate(
            (
                (al, out_al), (first, out_pr.at[:, pl.ds(0, 128), :]),
                (second, out_pr.at[low, half, :]), (done, out_pr.at[high, half, :]),
            )
        )
    ]
    loads[0].wait()

    def rest():
        for load in loads[1:]:
            load.wait()
        for store in stores[:3]:
            store.start()
        return old[...], gate[...]

    done[...] = finish(received, rest, cnt, swap_8, average, tow, tiw, tww, 8)
    stores[3].start()
    for store in stores:
        store.wait()


def kernel(
    pr_h, rmask_s_h, rmask_h, smask_h, pbw_h, tlw_h, trw_h, al_h, rwq_h, rwk_h, rwv_h, rwg_h, rwo_h, cwq_h, cwk_h, cwv_h, cwg_h, cwo_h, tgw_h, tow_h, tiw_h, tww_h,
    out_al, out_pr, out_second, out_c, out_gate,
    pn, lr_t, b_t, send_lr, recv_lr, recv_b, bias_t, send_m, recv_m, send_c, recv_c, send_q, recv_q,
    wt, wlr, qs, kz, vt, gs, gt, st, st_c, cn, gcol, cnt, gate, swap, swap_8, eye, average,
    al, rwq, rwk, rwv, rwg, rwo, cwq, cwk, cwv, cwg, cwo, tgw, tow, tiw, tww, al_v, pr_v, pr_w, pr, rmask_s, rmask, smask, pbw, tlw, trw,
    s_lr, r_lr, s_b, r_b, s_x, s_m, r_m, s_c, r_c, s_in, s_out, s_first,
):
    me = lax.axis_index("dap")

    def peer(o):
        return lax.rem(me + o, N)

    barrier = pltpu.get_barrier_semaphore()
    for o in range(1, N):
        pl.semaphore_signal(barrier, inc=1, device_id={"dap": peer(o)}, device_id_type=MESH)

    first_loads = [
        pltpu.make_async_copy(src, dst, s_first.at[n])
        for n, (src, dst) in enumerate(
            zip(
                (pr_h, tlw_h, trw_h, rmask_s_h, rmask_h, pbw_h, smask_h),
                (pr, tlw, trw, rmask_s, rmask, pbw, smask),
            )
        )
    ]
    loads = [
        pltpu.make_async_copy(src, dst, s_in.at[n])
        for n, (src, dst) in enumerate(
            zip(
                (rwq_h, rwv_h, rwg_h, cwq_h, cwv_h, cwg_h, tgw_h, al_h, rwk_h, rwo_h, cwk_h, cwo_h, tow_h, tiw_h, tww_h),
                (rwq, rwv, rwg, cwq, cwv, cwg, tgw, al, rwk, rwo, cwk, cwo, tow, tiw, tww),
            )
        )
    ]
    for load in first_loads:
        load.start()

    def copy(src, dst, ssem, rsem, to):
        return pltpu.make_async_remote_copy(
            src_ref=src, dst_ref=dst, send_sem=ssem, recv_sem=rsem,
            device_id={"dap": to}, device_id_type=MESH,
        )

    def send_to(send, recv, ssem, rsem, d):
        return copy(send.at[d], recv.at[me], ssem.at[d], rsem.at[me], d)

    def arrival(send, recv, ssem, rsem, d):
        return copy(send.at[d], recv.at[d], ssem.at[d], rsem.at[d], d)

    def wait_all(send, recv, ssem, rsem):
        @pl.loop(1, N)
        def _(o):
            arrival(send, recv, ssem, rsem, peer(o)).wait_recv()

    swap[...], swap_8[...], eye[...], average[...] = constants()

    for load in first_loads:
        load.wait()
    for load in loads:
        load.start()
    live = rmask[...].astype(F32)

    b_t[...] = jnp.zeros_like(b_t)
    normed_pair = normalize_rows(pr[...].reshape(4096, 128), average[...])
    pn[...] = normed_pair.reshape(16, 256, 128)
    heads = nt(pbw[...], normed_pair).astype(BF16)
    for i in range(16):
        b_t[i, :HEADS] = heads[:, i * 256 : i * 256 + 256]

    recv_b[me] = mm(swap[...], b_t[...].reshape(256, 256))[:128].astype(BF16).reshape(8, 16, 256)

    pl.semaphore_wait(barrier, N - 1)

    high = me // 8
    depth = lax.rem(me, 8)

    def along(dz):
        return high * 8 + lax.rem(depth + dz + 8, 8)

    across = lax.rem(me + 8, N)

    def pass_bias(n, origin, to):
        return copy(recv_b.at[origin], recv_b.at[origin], s_b.at[n], r_b.at[origin], to)

    def pass_across(origin):
        return copy(recv_b.at[origin], recv_b.at[origin], s_x.at[origin], r_b.at[origin], across)

    first_hops = [pass_bias(n, me, along(dz)) for n, dz in enumerate((1, -1, 2, -2))]
    second_hops = [
        pass_bias(4 + n, along(at), along(to)) for n, (at, to) in enumerate(((-2, 1), (2, -1), (-2, 2)))
    ]
    for hop in first_hops:
        hop.start()
    pass_across(me).start()

    wlr[:128, :] = transposed(tlw[...])
    wlr[128:, :] = transposed(trw[...])
    for i in range(16):
        own = rmask_s[me * 16 + i].astype(F32)
        lr_t[i] = (nt(wlr[...], pn[i]) * (live * own)).astype(BF16)

    def split_group(g):
        at = pl.multiple_of(g * 16, 16)
        for side in range(2):
            block = lr_t[:, pl.ds(side * 128 + at, 16), :].reshape(256, 256)
            swapped = mm(swap[...], block).astype(BF16).reshape(2, 8, 16, 256)
            send_lr[2 * g, side] = swapped[0]
            send_lr[2 * g + 1, side] = swapped[1]

    def send_group(n):
        g = lax.rem(me // 2 + n, 8)
        split_group(g)
        send_to(send_lr, recv_lr, s_lr, r_lr, 2 * g).start()
        send_to(send_lr, recv_lr, s_lr, r_lr, 2 * g + 1).start()

    @pl.loop(1, AHEAD)
    def _(n):
        send_group(n)

    for n, w in enumerate((rwq, rwv, rwg, cwq, cwv, cwg)):
        loads[n].wait()
        wt[n] = transposed(w[...])

    for dz in (2, -2, 1, -1):
        pass_across(along(dz)).wait_recv()
    for hop in second_hops:
        hop.start()
    for dz in (2, -2, 1, -1):
        pass_across(along(dz)).start()

    @pl.loop(AHEAD, 8)
    def _(n):
        send_group(n)

    split_group(me // 2)
    near = me + 1 - 2 * (me % 2)
    send_to(send_lr, recv_lr, s_lr, r_lr, near).start()
    recv_lr[me] = send_lr[me]

    vt[:, DH:, :] = jnp.ones((HEADS, 16, 256), BF16)

    loads[6].wait()

    gate[...] = sigmoid(mm(pn[...].reshape(4096, 128), tgw[...])).reshape(16, 256, 128)
    gate_out = pltpu.make_async_copy(gate.at[pl.ds(8, 8), pl.ds(128, 128), :], out_gate, s_out.at[3])
    gate_out.start()

    for dz in (3, -3, 4):
        pass_across(along(dz)).wait_recv()
        pass_across(along(dz)).start()
    for dz in range(8):
        pass_across((1 - high) * 8 + dz).wait_recv()
    shown = nt(eye[...], jnp.broadcast_to(live, (256, 256)).astype(BF16))
    hidden_keys = (1.0 - shown) * MASKED

    @pl.loop(0, HEADS, unroll=2)
    def _(h):
        bias_t[h] = nt(eye[...], recv_b[:, h].reshape(256, 256)) + hidden_keys

    scale = DH ** (-0.5)
    for load in loads[7:]:
        load.wait()

    lane_head = lax.broadcasted_iota(jnp.int32, (256, 256), 1) // DH

    def project(normed, first, wk):
        qs[...] = (nt(wt[first], normed) * scale).astype(BF16)
        v = nt(wt[first + 1], normed).astype(BF16)
        gs[...] = sigmoid(nt(wt[first + 2], normed))
        for h in range(HEADS):
            vt[h, :DH, :] = v[h * DH : (h + 1) * DH]
        return mm(normed, wk[...])

    def send_rows(n, d):
        some = pl.ds(4 * n, 4)
        return copy(send_m.at[d, some], recv_m.at[me, some], s_m.at[n, d], r_m.at[n, me], d)

    def row(s):
        k = project(normalize(al[s].astype(F32)), 0, rwk)
        for h in range(HEADS):
            kz[h * 256 : (h + 1) * 256, :] = jnp.where(lane_head == h, k, 0.0).astype(BF16)
        st[...] = mm(kz[...], qs[...])
        for h in range(HEADS):
            own = slice(h * DH, (h + 1) * DH)
            gt[own, :] = (attend(st[h * 256 : (h + 1) * 256, :], bias_t[h], vt[h]) * gs[own, :]).astype(BF16)
        mid = (al[s].astype(F32) + tn(gt[...], rwo[...])).astype(BF16)
        send_m[:, s] = mid.reshape(16, 16, 256)

    for n in range(2):
        pl.loop(4 * n, 4 * n + 4)(row)
        for o in range(1, N):
            send_rows(n, peer(o)).start()

    recv_m[me] = send_m[me]

    wait_all(send_lr, recv_lr, s_lr, r_lr)

    sources = (send_c, send_q.at[0], send_q.at[1])
    targets = (recv_c, recv_q, out_c)

    def send_part(n, d):
        return copy(sources[n].at[d], targets[n].at[me], s_c.at[n, d], r_c.at[n, me], d)

    def product(c, n):
        left = recv_lr[:, 0, c].reshape(256, 256)
        return nt(left, recv_lr[n * 8 : n * 8 + 8, 1, c].reshape(128, 256))

    @pl.loop(0, 8, unroll=2)
    def _(c):
        send_c[:, c] = product(c, 0).astype(BF16).reshape(16, 16, 128)

    for o in range(1, N):
        send_part(0, peer(o)).start()

    @pl.loop(0, 4)
    def _(c):
        even = product(2 * c, 1).reshape(16, 2, 8, 128)
        odd = product(2 * c + 1, 1).reshape(16, 2, 8, 128)
        for q in range(2):
            send_q[q, :, c] = jnp.concatenate([even[:, q], odd[:, q]], axis=1).astype(BF16)

    for n in (1, 2):
        for o in range(1, N):
            send_part(n, peer(o)).start()
    recv_c[me] = send_c[me]
    recv_q[me] = send_q[0, me]
    own_c = pltpu.make_async_copy(send_q.at[1, me], out_c.at[me], s_out.at[2])
    own_c.start()

    @pl.loop(1, N)
    def _(o):
        d = peer(o)
        for n in range(2):
            some = pl.ds(4 * n, 4)
            copy(send_m.at[d, some], recv_m.at[d, some], s_m.at[n, d], r_m.at[n, d], d).wait_recv()


    @pl.loop(0, 8)
    def _(b):
        rows = recv_m[pl.ds(2 * b, 2)].reshape(256, 256).astype(F32)
        at = pl.multiple_of(b * 16, 16)
        cn[:, pl.ds(at, 16), :] = mm(swap[...], normalize(rows)).astype(BF16).reshape(16, 16, 256)

    seen = nt(eye[:128, :128], jnp.broadcast_to(smask[...].astype(F32), (128, 128)).astype(BF16))
    hidden_rows = (1.0 - seen) * MASKED

    @pl.loop(0, 8)
    def _(p):
        k = project(cn[pl.ds(2 * p, 2)].reshape(256, 256), 3, cwk)
        for h in range(HEADS):
            one = jnp.where(lane_head == h, k, 0.0).astype(BF16)
            kz[h * 128 : (h + 1) * 128, :] = one[:128]
            kz[1024 + h * 128 : 1024 + (h + 1) * 128, :] = one[128:]
        for n in range(2):
            half = slice(n * 128, n * 128 + 128)
            st_c[n] = mm(kz[n * 1024 : (n + 1) * 1024, :], qs[:, half])
        for n in range(2):
            half = slice(n * 128, n * 128 + 128)
            for h in range(HEADS):
                own = slice(h * DH, (h + 1) * DH)
                mixed = attend(st_c[n, h * 128 : (h + 1) * 128, :], hidden_rows, vt[h, :, half])
                gt[own, half] = (mixed * gs[own, half]).astype(BF16)
        for n in range(2):
            gcol[2 * p + n] = transposed(gt[:, n * 128 : n * 128 + 128])

    @pl.loop(0, 8)
    def _(b):
        at = pl.multiple_of(b * 16, 16)
        rows = mm(swap[...], gcol[:, pl.ds(at, 16), :].reshape(256, 256)).astype(BF16)
        mid = recv_m[pl.ds(2 * b, 2)].reshape(256, 256).astype(F32)
        al_v[pl.ds(at, 16)] = (mid + mm(rows, cwo[...])).astype(BF16).reshape(16, 16, 256)

    out_rows = pltpu.make_async_copy(al_v, out_al, s_out.at[0])
    out_rows.start()

    def wait_part(n):
        @pl.loop(1, N)
        def _(o):
            d = peer(o)
            copy(sources[n].at[d], targets[n].at[d], s_c.at[n, d], r_c.at[n, d], d).wait_recv()

    wait_part(0)
    pr_v[...] = finish(
        recv_c, lambda: (pr[:, :128, :], gate[:, :128, :]), cnt, swap[...], average[...], tow, tiw, tww, 16
    )
    pair_out = pltpu.make_async_copy(pr_v, out_pr, s_out.at[1])
    pair_out.start()
    wait_part(1)
    pr_w[...] = finish(
        recv_q, lambda: (pr[:8, 128:, :], gate[:8, 128:, :]), cnt, swap_8[...], average[...], tow, tiw, tww, 8
    )
    second_out = pltpu.make_async_copy(pr_w, out_second, s_out.at[4])
    second_out.start()
    wait_part(2)

    for hop in first_hops + second_hops:
        hop.wait_send()
    for dz in range(8):
        pass_across(high * 8 + dz).wait_send()

    @pl.loop(1, N)
    def _(o):
        d = peer(o)
        send_to(send_lr, recv_lr, s_lr, r_lr, d).wait_send()
        send_rows(0, d).wait_send()
        send_rows(1, d).wait_send()
        for n in range(3):
            send_part(n, d).wait_send()

    for done in (out_rows, pair_out, second_out, own_c, gate_out):
        done.wait()


def shards(
    alignment, pair_state, residue_present_mask, alignment_row_mask,
    row_query_weight, row_key_weight, row_value_weight, row_gate_weight, row_output_weight,
    pair_bias_weight,
    column_query_weight, column_key_weight, column_value_weight, column_gate_weight, column_output_weight,
    triangle_left_weight, triangle_right_weight, triangle_gate_weight, triangle_output_weight,
    transition_input_weight, transition_output_weight,
):
    hbm = pl.BlockSpec(memory_space=pl.ANY)
    dma = pltpu.SemaphoreType.DMA((N,))
    al_done, first, second, received, gates = (
        pl.pallas_call(
            kernel,
            out_shape=(
                jax.ShapeDtypeStruct((128, 16, 256), BF16),
                jax.ShapeDtypeStruct((16, 128, 128), BF16),
                jax.ShapeDtypeStruct((8, 128, 128), BF16),
                jax.ShapeDtypeStruct((N, 4, 16, 128), BF16),
                jax.ShapeDtypeStruct((8, 128, 128), F32),
            ),
            in_specs=[hbm] * 22,
            out_specs=(hbm,) * 5,
            scratch_shapes=[
                pltpu.VMEM((16, 256, 128), BF16),
                pltpu.VMEM((16, 256, 256), BF16),
                pltpu.VMEM((16, 16, 256), BF16),
                pltpu.VMEM((N, 2, 8, 16, 256), BF16),
                pltpu.VMEM((N, 2, 8, 16, 256), BF16),
                pltpu.VMEM((N, 8, 16, 256), BF16),
                pltpu.VMEM((8, 256, 256), F32),
                pltpu.VMEM((N, 8, 16, 256), BF16),
                pltpu.VMEM((N, 8, 16, 256), BF16),
                pltpu.VMEM((N, 8, 16, 128), BF16),
                pltpu.VMEM((N, 8, 16, 128), BF16),
                pltpu.VMEM((2, N, 4, 16, 128), BF16),
                pltpu.VMEM((N, 4, 16, 128), BF16),
                pltpu.VMEM((6, 256, 256), BF16),
                pltpu.VMEM((256, 128), BF16),
                pltpu.VMEM((256, 256), BF16),
                pltpu.VMEM((2048, 256), BF16),
                pltpu.VMEM((8, 48, 256), BF16),
                pltpu.VMEM((256, 256), F32),
                pltpu.VMEM((256, 256), BF16),
                pltpu.VMEM((2048, 256), F32),
                pltpu.VMEM((2, 1024, 128), F32),
                pltpu.VMEM((16, 128, 256), BF16),
                pltpu.VMEM((16, 128, 256), BF16),
                pltpu.VMEM((16, 128, 128), BF16),
                pltpu.VMEM((16, 256, 128), F32),
                pltpu.VMEM((256, 256), BF16),
                pltpu.VMEM((256, 256), BF16),
                pltpu.VMEM((256, 256), BF16),
                pltpu.VMEM((128, 128), BF16),
            ]
            + [pltpu.VMEM((8, 256, 256), BF16)]
            + [pltpu.VMEM((256, 256), BF16)] * 10
            + [pltpu.VMEM((128, 128), BF16)] * 2
            + [
                pltpu.VMEM((128, 512), BF16),
                pltpu.VMEM((512, 128), BF16),
                pltpu.VMEM((128, 16, 256), BF16),
                pltpu.VMEM((16, 128, 128), BF16),
                pltpu.VMEM((8, 128, 128), BF16),
                pltpu.VMEM((16, 256, 128), BF16),
                pltpu.SMEM((256,), jnp.int32),
                pltpu.VMEM((1, 256), jnp.int32),
                pltpu.VMEM((1, 128), jnp.int32),
                pltpu.VMEM((8, 128), BF16),
                pltpu.VMEM((128, 128), BF16),
                pltpu.VMEM((128, 128), BF16),
            ]
            + [dma] * 5
            + [pltpu.SemaphoreType.DMA((2, N))] * 2
            + [pltpu.SemaphoreType.DMA((3, N))] * 2
            + [dma, pltpu.SemaphoreType.DMA((5,)), pltpu.SemaphoreType.DMA((7,))],
            compiler_params=pltpu.CompilerParams(
                collective_id=0, has_side_effects=True, vmem_limit_bytes=56 << 20
            ),
        )(
            pair_state, residue_present_mask,
            residue_present_mask.reshape(1, 256), alignment_row_mask.reshape(1, 128),
            pair_bias_weight.T, triangle_left_weight, triangle_right_weight,
            alignment,
            row_query_weight, row_key_weight, row_value_weight, row_gate_weight, row_output_weight,
            column_query_weight, column_key_weight, column_value_weight, column_gate_weight,
            column_output_weight,
            triangle_gate_weight, triangle_output_weight,
            transition_input_weight, transition_output_weight,
        )
    )
    return tuple(
        pl.pallas_call(
            last_part,
            out_shape=(
                jax.ShapeDtypeStruct((128, 16, 256), BF16),
                jax.ShapeDtypeStruct((16, 256, 128), BF16),
            ),
            in_specs=[hbm] * 9,
            out_specs=(hbm, hbm),
            scratch_shapes=[
                pltpu.VMEM((128, 16, 256), BF16),
                pltpu.VMEM((16, 128, 128), BF16),
                pltpu.VMEM((8, 128, 128), BF16),
                pltpu.VMEM((N, 4, 16, 128), BF16),
                pltpu.VMEM((8, 128, 128), F32),
                pltpu.VMEM((8, 128, 128), BF16),
                pltpu.VMEM((128, 128), BF16),
                pltpu.VMEM((128, 512), BF16),
                pltpu.VMEM((512, 128), BF16),
                pltpu.VMEM((8, 128, 128), BF16),
                pltpu.VMEM((8, 128, 128), BF16),
                pltpu.SemaphoreType.DMA((9,)),
                pltpu.SemaphoreType.DMA((4,)),
            ],
            compiler_params=pltpu.CompilerParams(vmem_limit_bytes=56 << 20),
        )(
            al_done, first, second, received, gates, pair_state,
            triangle_output_weight, transition_input_weight, transition_output_weight,
        )
    )


def solution(mesh):
    in_specs = (
        P(("dp", "dap"), None, None),
        P(("dp", "dap"), None, None),
        P("dp"),
        P("dp"),
    ) + (P(),) * 17
    out_specs = (P("dp", "dap", None), P(("dp", "dap"), None, None))
    return jax.shard_map(shards, mesh=mesh, in_specs=in_specs, out_specs=out_specs, check_vma=False)
```
